128 devices in a mesh: scen: 32 (over z, y, x_lo), asset: 4 (over x_hi, core).
Axes of the slice: x: 4 (x_hi: 2, x_lo: 2; x = x_hi * 2 + x_lo), y: 4, z: 4, core: 2. Of those that a mesh axis runs over, the one named last changes fastest.
Arguments:
- returns: bfloat16 [196608, 6144], P('scen', 'asset'), may hold values from -1 to 1
- mean_return: float32 [6144], P('asset'), may hold values from -1 to 2
- targets: float32 [64], replicated, may hold values from 0.2 to 0.8
- weights: float32 [64, 6144], P(None, 'asset'), may hold values from 0 to 12
- threshold: float32 [64], replicated, may hold values from 0 to 1
- hinge_duals: float32 [64, 196608], P(None, 'scen'), may hold values from 0 to 1
- multiplier: float32 [64], replicated, may hold values from 0 to 0.5
Outputs:
- weights_out: float32 [64, 6144], P(None, 'asset')
- threshold_out: float32 [64], replicated
- duals_out: float32 [64, 196608], P(None, 'scen')
- multiplier_out: float32 [64], replicated
- tail_risk: float32 [64], replicated
The draws below stay inside these ranges and needn't reach their ends.
All inputs are finite; a program needn't handle non-finite values.
Results may differ from the reference program's by a relative error of at most 0.006.
The reference program's roundings to bfloat16 on the way count: a program that leaves them out, or rounds other values in their place, can miss the bound.
Values sent between devices are 32-bit elements; how exact they have to be, the bound alone decides.
No kernel may reach another device: no remote copies, remote signals or barrier semaphores. Data moves between devices by JAX's collectives and lax.ppermute only.
A program may use at most 128 MiB of HBM per device.

```python
import math
import jax
import jax.numpy as jnp
from jax import lax

K = 64
N = 6144
SCEN_DEV = 6144
BISECT = 6
ITERS = 2
S = 196608
N_SCEN = 32


def draw_returns(key, part):
    key = jax.random.fold_in(key, 7)
    noise_key, row_key, col_key = jax.random.split(key, 3)
    position = jnp.arange(S, dtype=jnp.float32) / max(S - 1, 1)
    trend = jnp.exp(position * math.log(3.0))
    col_scale = jnp.exp(jax.random.uniform(col_key, (1, N), jnp.float32, 0.0, math.log(10.0)))
    row_scale = trend * jnp.exp(jax.random.uniform(row_key, (S,), jnp.float32, 0.0, math.log(10.0 / 3.0)))
    base = jnp.clip(jax.random.normal(noise_key, (S, N), jnp.float32), -6.0, 6.0)
    divisor = 8.0
    values = base * row_scale[:, None] * col_scale / (divisor * math.sqrt(N))
    return jnp.clip(values, -1.0, 1.0).astype(jnp.bfloat16)


def draw_weights(key, part):
    key = jax.random.fold_in(key, 11)
    column = jnp.arange(N, dtype=jnp.float32) / max(N - 1, 1)
    rising = jnp.exp(column * math.log(3.0))
    spread = jnp.exp(jax.random.uniform(key, (K, N), jnp.float32, math.log(0.25), math.log(2.0)))
    return (spread * rising[None, :]).astype(jnp.float32)


def block_scale(rng, dims, cuts, low, high):
    factor_of = 1.0
    for dim, parts in cuts:
        heights = jax.random.uniform(jax.random.fold_in(jax.random.fold_in(rng, 6), dim), (parts,), jnp.float32, low / len(cuts), high / len(cuts))
        factor_of = factor_of * jnp.repeat(jnp.exp(heights), dims[dim] // parts).reshape((-1,) + (1,) * (len(dims) - 1 - dim))
    return factor_of


def setup_inputs(seed: int = 0) -> dict:
    streams_of = jax.random.split(jax.random.key(seed), 8)
    return {
        "returns": draw_returns(jax.random.fold_in(streams_of[7], 71), 0),
        "mean_return": jnp.clip(-1.0 + 3.0 * jax.random.uniform(streams_of[1], (N,), jnp.float32) ** block_scale(streams_of[1], (N,), ((0, 4),), -0.2, 0.2), -1.0, 2.0),
        "targets": jnp.clip(jax.random.uniform(streams_of[2], (K,), jnp.float32, 0.2, 0.8), 0.2, 0.8),
        "weights": draw_weights(jax.random.fold_in(streams_of[7], 71), 0),
        "threshold": jnp.clip(jax.random.uniform(streams_of[4], (K,), jnp.float32, 0.0, 1.0), 0.0, 1.0),
        "hinge_duals": jnp.clip(1.0 * jax.random.uniform(streams_of[5], (K, S), jnp.float32) ** block_scale(streams_of[5], (K, S), ((1, 32),), -0.2, 0.2), 0.0, 1.0),
        "multiplier": jnp.clip(jax.random.uniform(streams_of[6], (K,), jnp.float32, 0.0, 0.5), 0.0, 0.5),
    }


TAIL = 0.2
STEP_V = 1.0
STEP_T = 0.5
STEP_U = 0.5
STEP_L = 2.0

def grad_sum(dual_bf, returns):
    blocks = returns.reshape(N_SCEN, SCEN_DEV, N)
    dual_blocks = dual_bf.reshape(K, N_SCEN, SCEN_DEV).transpose(1, 0, 2)

    def add_block(running, pair):
        block, dual_block = pair
        return (running + jnp.dot(dual_block, block, preferred_element_type=jnp.float32), None)
    running, _ = lax.scan(add_block, jnp.zeros((K, N), jnp.float32), (blocks, dual_blocks))
    return running

def losses(alloc_bf, returns):
    blocks = returns.reshape(N_SCEN, SCEN_DEV, N)

    def block_loss(block):
        return -lax.dot_general(alloc_bf, block, (((1,), (1,)), ((), ())), preferred_element_type=jnp.float32)
    stacked = lax.map(block_loss, blocks)
    return stacked.transpose(1, 0, 2).reshape(K, S)

def project(matrix):
    lower = lax.optimization_barrier(jnp.sum(matrix, 1)) / N - 1.0
    upper = lax.optimization_barrier(jnp.max(matrix, 1))
    f_low = lax.optimization_barrier(jnp.sum(jnp.maximum(matrix - lower[:, None], 0.0), 1)) - N
    f_up = jnp.zeros_like(lower) - N

    def sweep_once(index, bounds):
        lower, upper, f_low, f_up = bounds
        middle = (lower + upper) * 0.5
        excess = lax.optimization_barrier(jnp.sum(jnp.maximum(matrix - middle[:, None], 0.0), 1)) - N
        raise_low = excess >= 0
        return (jnp.where(raise_low, middle, lower), jnp.where(raise_low, upper, middle), jnp.where(raise_low, excess, f_low), jnp.where(raise_low, f_up, excess))
    lower, upper, f_low, f_up = lax.fori_loop(0, BISECT, sweep_once, (lower, upper, f_low, f_up))
    theta = lower + f_low * (upper - lower) / (f_low - f_up)
    return jnp.maximum(matrix - theta[:, None], 0.0)

def operate(current, returns, mean_return, targets):
    weights, threshold, hinge_duals, multiplier = current
    gradient = grad_sum(hinge_duals.astype(jnp.bfloat16), returns)
    step_scale = math.sqrt(N / S)
    shifted = weights + STEP_V * (step_scale * gradient + multiplier[:, None] * mean_return[None, :])
    new_weights = project(shifted)
    new_threshold = threshold - STEP_T * (1.0 - lax.optimization_barrier(jnp.sum(hinge_duals, 1)) / S / TAIL)
    bar_weights = 2.0 * new_weights - weights
    bar_threshold = 2.0 * new_threshold - threshold
    loss = losses(bar_weights.astype(jnp.bfloat16), returns)
    expected = lax.optimization_barrier(jnp.sum(bar_weights * mean_return[None, :], 1)) / N
    new_duals = jnp.clip(hinge_duals + STEP_U * (loss - bar_threshold[:, None]), 0.0, 1.0)
    new_multiplier = jnp.maximum(multiplier + STEP_L * (targets - expected), 0.0)
    return (new_weights, new_threshold, new_duals, new_multiplier)

def reference(returns, mean_return, targets, weights, threshold, hinge_duals, multiplier):
    anchor = (weights, threshold, hinge_duals, multiplier)
    current = anchor
    for sweep in range(ITERS):
        updated = operate(current, returns, mean_return, targets)
        weight_old = (sweep + 1.0) / (sweep + 2.0)
        current = tuple((weight_old * (2.0 * fresh_part - old_part) + start_part / (sweep + 2.0) for fresh_part, old_part, start_part in zip(updated, current, anchor)))
    weights_out, threshold_out, duals_out, multiplier_out = current
    tail_loss = losses(weights_out.astype(jnp.bfloat16), returns)
    hinge_sums = lax.optimization_barrier(jnp.sum(jnp.maximum(tail_loss - threshold_out[:, None], 0.0), 1))
    tail_risk = threshold_out + hinge_sums / (TAIL * S)
    return (weights_out, threshold_out, duals_out, multiplier_out, tail_risk)
```

```python
import math

import jax
import jax.numpy as jnp
from jax import lax
from jax.experimental import pallas as pl
from jax.experimental.pallas import tpu as pltpu
from jax.sharding import Mesh
from jax.sharding import PartitionSpec as P

BISECT = 6
TAIL = 0.2
STEP_V = 1.0
STEP_T = 0.5
STEP_U = 0.5
STEP_L = 2.0

SCEN = ("z", "y", "xl")
ASSET = ("xh", "core")
ALL = SCEN + ASSET

K = 64
HALF = 32
LANES = 128
TILE = 768

F32 = jnp.float32
BF16 = jnp.bfloat16

VMEM = pl.BlockSpec(memory_space=pltpu.VMEM)
SMEM = pl.BlockSpec(memory_space=pltpu.SMEM)
ANY = pl.BlockSpec(memory_space=pl.ANY)


def params():
    return pltpu.CompilerParams(vmem_limit_bytes=12 << 20)


def shape(*dims, dtype=F32):
    return jax.ShapeDtypeStruct(dims, dtype)


def cost(macs, nbytes):
    return pl.CostEstimate(flops=2 * macs, bytes_accessed=nbytes, transcendentals=0)


def start_of(offset):
    return pl.multiple_of(offset, LANES)


def lane_folded(values):
    total = values[:, 0:LANES]
    for j in range(1, values.shape[1] // LANES):
        total = total + values[:, j * LANES : (j + 1) * LANES]
    return total


def row_total(folded):
    return jnp.broadcast_to(jnp.sum(folded, 1, keepdims=True), folded.shape)


def diagonal(rows, first=0):
    return lax.broadcasted_iota(jnp.int32, (rows, LANES), 1) == first + lax.broadcasted_iota(
        jnp.int32, (rows, LANES), 0
    )


def in_lanes(column):
    return jnp.sum(jnp.where(diagonal(K), column, 0.0), 0, keepdims=True)[:, 0:K]


def in_rows(line):
    square = diagonal(K)[:, 0:K]
    return jnp.sum(jnp.where(square, jnp.broadcast_to(line, (K, K)), 0.0), 1, keepdims=True)


def picked(line, row):
    at = lax.broadcasted_iota(jnp.int32, line.shape, 1) == row
    return jnp.sum(jnp.where(at, line, 0.0), 1, keepdims=True)


def row_base(core_side, quarter, width):
    core = lax.axis_index("core")
    half = core if core_side else 1 - core
    return start_of((half * 2 + quarter) * width)


def scen_index():
    return (lax.axis_index("z") * 4 + lax.axis_index("y")) * 2 + lax.axis_index("xl")


def call(body, name, operands, outs, macs=0, nbytes=0, scratch=(), in_specs=None):
    single = not isinstance(outs, list)
    return pl.pallas_call(
        body,
        in_specs=in_specs or [VMEM] * len(operands),
        out_specs=VMEM if single else [VMEM] * len(outs),
        out_shape=outs,
        scratch_shapes=list(scratch),
        compiler_params=params(),
        cost_estimate=cost(macs, nbytes),
        name=name,
    )(*operands)


def pack(acc, mass, out):
    blocks = acc.shape[1] // LANES
    for j in range(blocks):
        out[:, j, :] = acc[0:HALF, j * LANES : (j + 1) * LANES]
        out[:, blocks + j, :] = acc[HALF:K, j * LANES : (j + 1) * LANES]
    out[:, 2 * blocks, :] = mass[0:HALF, :]
    out[:, 2 * blocks + 1, :] = mass[HALF:K, :]
    for j in range(2 * blocks + 2, out.shape[1]):
        out[:, j, :] = jnp.zeros((HALF, LANES), F32)


def first_gradient(duals, returns):
    rows, cols = returns.shape
    steps = rows // TILE

    def body(u, r, out, held, kept, acc, sems, dual_sems):
        copies = []
        for i in range(steps):
            at = pl.ds(i * TILE, TILE)
            mine = pltpu.make_async_copy(u.at[:, at], kept.at[:, at], dual_sems.at[i])
            block = pltpu.make_async_copy(r.at[at], held.at[at], sems.at[i])
            mine.start()
            block.start()
            copies.append((mine, block))
        folded = jnp.zeros((K, LANES), F32)
        for i in range(steps):
            copies[i][0].wait()
            part = kept[:, i * TILE : (i + 1) * TILE]
            folded = folded + lane_folded(part)
            copies[i][1].wait()
            term = jnp.dot(
                part.astype(BF16), held[pl.ds(i * TILE, TILE), :], preferred_element_type=F32
            )
            acc[...] = term if i == 0 else acc[...] + term
        pack(acc[...], row_total(folded), out)

    operands = [pltpu.with_memory_space_constraint(a, pltpu.HBM) for a in (duals, returns)]
    outs = [shape(HALF, HALF, LANES), pltpu.VMEM((rows, cols), BF16), pltpu.VMEM((K, rows), F32)]
    scratch = (
        pltpu.VMEM((K, cols), F32),
        pltpu.SemaphoreType.DMA((steps,)),
        pltpu.SemaphoreType.DMA((steps,)),
    )
    return call(
        body, "first_gradient", operands, outs, K * rows * cols, 2 * rows * cols, scratch, [ANY, ANY]
    )


def own_rows(received, state, t_old, extra, first, total_cols, total_rows):
    scale = math.sqrt(total_cols / total_rows)
    cols = state.shape[1]
    blocks = cols // LANES

    def body(got, v, t, more, out):
        s = scen_index()
        grad = jnp.sum(got[...], 0)
        out[2 * blocks : HALF, :] = jnp.zeros((HALF - 2 * blocks, LANES), F32)
        for half in range(2):
            values = v[half * HALF : (half + 1) * HALF, :]
            at = lax.broadcasted_iota(jnp.int32, values.shape, 0) == s
            old = jnp.sum(jnp.where(at, values, 0.0), 0, keepdims=True)
            for j in range(blocks):
                line = half * blocks + j
                out[line : line + 1, :] = (
                    old[:, j * LANES : (j + 1) * LANES] + STEP_V * scale * grad[line : line + 1, :]
                )
                if first:
                    out[HALF + line : HALF + line + 1, :] = more[:, j * LANES : (j + 1) * LANES]
            line = 2 * blocks + half
            out[line : line + 1, :] = picked(t[...], s + half * HALF) - STEP_T * (
                1.0 - grad[line : line + 1, :] / total_rows / TAIL
            )
        if not first:
            out[2 * blocks + 2 : 2 * blocks + 3, 0:K] = more[...]

    return call(
        body,
        "own_rows",
        (received, state, t_old, extra),
        shape(HALF + 2 * blocks if first else HALF, LANES),
        nbytes=4 * HALF * HALF * LANES,
    )


def projected(gathered, own, gathered_first, own_first, lam_old, goal, first, total_cols):
    lines = (gathered_first.shape[1] - HALF) // 2 * 2
    blocks = lines // 2

    def body(rows, mine, means, mean, lam_in, target, out, lam_out):
        s = scen_index()
        first_row = lax.broadcasted_iota(jnp.int32, (lines, LANES), 0) < blocks

        def sums(values):
            a = jnp.sum(jnp.where(first_row, values, 0.0), (0, 1), keepdims=True)
            b = jnp.sum(jnp.where(first_row, 0.0, values), (0, 1), keepdims=True)
            return jnp.concatenate([a, b], 0)

        def spread(pair):
            return jnp.where(first_row, pair[0:1, :], pair[1:2, :])

        lam = lam_in[...]
        if not first:
            ret = rows[0, lines + 2 : lines + 3, 0:K]
            for i in range(1, rows.shape[0]):
                ret = ret + rows[i, lines + 2 : lines + 3, 0:K]
            lam = jnp.maximum(lam + STEP_L * (target[...] - ret / total_cols), 0.0)
        lam_out[...] = lam
        slope = STEP_V * spread(jnp.concatenate([picked(lam, s), picked(lam, s + HALF)], 0))
        parts = [
            rows[i, 0:lines, :] + slope * means[i, HALF : HALF + lines, :]
            for i in range(rows.shape[0])
        ]
        total = parts[0]
        top = parts[0]
        for part in parts[1:]:
            total = total + part
            top = jnp.maximum(top, part)
        low = jnp.min(top, (0, 1), keepdims=True)
        top_a = jnp.max(jnp.where(first_row, top, low), (0, 1), keepdims=True)
        top_b = jnp.max(jnp.where(first_row, low, top), (0, 1), keepdims=True)
        upper = jnp.concatenate([top_a, top_b], 0)
        lower = sums(total) / total_cols - 1.0

        def excess_at(level):
            wide = spread(level)
            over = jnp.maximum(parts[0] - wide, 0.0)
            for part in parts[1:]:
                over = over + jnp.maximum(part - wide, 0.0)
            return sums(over) - total_cols

        f_low = excess_at(lower)
        f_up = jnp.zeros_like(lower) - total_cols
        for _ in range(BISECT):
            middle = (lower + upper) * 0.5
            excess = excess_at(middle)
            raise_low = excess >= 0
            lower = jnp.where(raise_low, middle, lower)
            upper = jnp.where(raise_low, upper, middle)
            f_low = jnp.where(raise_low, excess, f_low)
            f_up = jnp.where(raise_low, f_up, excess)
        theta = lower + f_low * (upper - lower) / (f_low - f_up)
        x = mine[0:lines, :] + slope * mean[HALF : HALF + lines, :]
        fresh = jnp.maximum(x - spread(theta), 0.0)
        rest = mine[lines:HALF, :]
        for i in range(HALF):
            out[i, 0:lines, :] = fresh
            out[i, lines:HALF, :] = rest

    return call(
        body,
        "projected",
        (gathered, own, gathered_first, own_first, lam_old, goal),
        [shape(HALF, HALF, LANES), shape(1, K)],
        nbytes=4 * HALF * HALF * LANES,
    )


def unpacked(received, state, start, mean_row, t_old, last):
    cols = state.shape[1]
    blocks = cols // LANES

    def body(got, v, w, m, t, fresh, bars, t_new, t_bar, ret, *mixed):
        for j in range(blocks):
            at = slice(j * LANES, (j + 1) * LANES)
            fresh[0:HALF, at] = got[:, j, :]
            fresh[HALF:K, at] = got[:, blocks + j, :]
        column = jnp.concatenate([got[:, 2 * blocks, :], got[:, 2 * blocks + 1, :]], 0)
        t_new[...] = in_lanes(column)
        t_bar[...] = 2.0 * column - in_rows(t[...])
        bar = 2.0 * fresh[...] - v[...]
        bars[0:K, :] = (-bar).astype(BF16)
        if not last:
            bars[K : 2 * K, :] = (-w[...]).astype(BF16)
        else:
            mixed[0][...] = (2.0 / 3.0) * bar + w[...] / 3.0
        ret[...] = in_lanes(row_total(lane_folded(bar * m[...])))

    outs = [
        shape(K, cols),
        shape((1 if last else 2) * K, cols, dtype=BF16),
        shape(1, K),
        shape(K, LANES),
        shape(1, K),
    ]
    if last:
        outs.append(shape(K, cols))
    return call(
        body, "unpacked", (received, state, start, mean_row, t_old), outs, nbytes=20 * K * cols
    )


def loss_part(bars, returns, side, quarter, width):
    cols = returns.shape[1]
    count = bars.shape[0] // K

    def body(b, r, *outs):
        base = row_base(side, quarter(), width)
        for i in range(width // TILE):
            at = slice(i * TILE, (i + 1) * TILE)
            block = r[pl.ds(start_of(base + i * TILE), TILE), :]
            term = lax.dot_general(
                block, b[...], (((1,), (1,)), ((), ())), preferred_element_type=F32
            ).T
            for part in range(count):
                outs[part][:, at] = term[part * K : (part + 1) * K, :]

    return call(
        body,
        "loss_part",
        (bars, returns),
        [shape(K, width)] * count,
        count * K * width * cols,
        2 * width * cols,
    )


def plus(a, b):
    def body(x, y, out):
        out[...] = x[...] + y[...]

    return call(body, "plus", (a, b), shape(*a.shape), nbytes=12 * a.size)


def own_and_other(keeps, takes):
    def body(k0, t0, k1, t1, send, keep):
        near = k0[...] + t0[...]
        far = k1[...] + t1[...]
        swap = lax.axis_index("xh") == 0
        send[...] = jnp.where(swap, far, near)
        keep[...] = jnp.where(swap, near, far)

    return call(
        body,
        "own_and_other",
        (keeps[0], takes[0], keeps[1], takes[1]),
        [shape(*keeps[0].shape)] * 2,
        nbytes=24 * keeps[0].size,
    )


def dual_step(loss, duals, t_bar):
    return jnp.clip(duals + STEP_U * (loss - t_bar[:, 0:1]), 0.0, 1.0)


def dual_rows(part, other, duals, t_bar, quarter, width):
    def body(p, o, u, t, fresh):
        base = row_base(1, quarter, width)
        fresh[...] = dual_step(p[...] + o[...], u[:, pl.ds(base, width)], t[...])

    return call(
        body, "dual_rows", (part, other, duals, t_bar), shape(K, width), nbytes=16 * K * width
    )


def gradient_part(terms, returns, before, width):
    cols = returns.shape[1]
    count = len(terms)

    def body(r, *refs):
        fed, rest = refs[:count], refs[count:]
        acc_out, folded_out = rest[-2:]
        total = rest[0][...] if before else None
        folds = rest[1][...] if before else None
        for (_, side, quarter), ref in zip(terms, fed):
            base = row_base(side, quarter, width)
            value = ref[...]
            term = jnp.dot(
                value.astype(BF16), r[pl.ds(base, width), :], preferred_element_type=F32
            )
            total = term if total is None else total + term
            fold = lane_folded(value)
            folds = fold if folds is None else folds + fold
        acc_out[...] = total
        folded_out[...] = folds

    operands = [returns] + [values for values, _, _ in terms] + list(before)
    return call(
        body,
        "gradient_part",
        operands,
        [shape(K, cols), shape(K, LANES)],
        count * K * width * cols,
        2 * count * width * cols,
    )


def gradient_end(taken, side, quarter, returns, before, width):
    cols = returns.shape[1]

    def body(r, got, acc_in, folded_in, out):
        base = row_base(side, quarter, width)
        term = acc_in[...] + jnp.dot(
            got[...].astype(BF16), r[pl.ds(base, width), :], preferred_element_type=F32
        )
        pack(term, row_total(folded_in[...] + lane_folded(got[...])), out)

    return call(
        body,
        "gradient_end",
        (returns, taken, *before),
        shape(HALF, HALF, LANES),
        K * width * cols,
        2 * width * cols,
    )


def final_duals(part, other, tails, held, start, t_new, t_old, t_start, t_bar, ret, width):
    devices = 128

    def body(p, o, la, lb, ua, ub, u0, tn, t, ts, tb, er, duals_out, t_out, sums):
        mine = lax.axis_index("xh")
        base = row_base(1, mine, width)
        loss = p[...] + o[...]
        old = jnp.where(mine == 0, ua[...], ub[...])
        fresh = dual_step(loss, old, tb[...])
        duals_out[...] = (2.0 / 3.0) * (2.0 * fresh - old) + u0[:, pl.ds(base, width)] / 3.0
        end = (2.0 / 3.0) * (2.0 * tn[...] - t[...]) + ts[...] / 3.0
        t_out[...] = end
        tail = (2.0 / 3.0) * loss + (la[...] + lb[...]) / 3.0
        over = jnp.maximum(tail - in_rows(end), 0.0)
        line = jnp.concatenate([in_lanes(row_total(lane_folded(over))), er[...]], 1)
        sums[...] = jnp.broadcast_to(line[None], (devices, 1, LANES))

    operands = (part, other, *tails, *held, start, t_new, t_old, t_start, t_bar, ret)
    return call(
        body,
        "final_duals",
        operands,
        [shape(K, width), shape(1, K), shape(devices, 1, LANES)],
        nbytes=24 * K * width,
    )


def joined(pieces, width):
    def body(far_near, near, far, own, out):
        mine = lax.axis_index("xh")
        out[:, pl.ds(row_base(0, 1 - mine, width), width)] = far_near[...]
        out[:, pl.ds(row_base(1, 1 - mine, width), width)] = near[...]
        out[:, pl.ds(row_base(0, mine, width), width)] = far[...]
        out[:, pl.ds(row_base(1, mine, width), width)] = own[...]

    return call(body, "joined", pieces, shape(K, 4 * width), nbytes=32 * K * width)


def finished(sums, t_out, lam, lam_start, goal, total_cols, total_rows):
    devices = sums.shape[0]
    copies = devices // 4

    def body(got, end, lam_old, lam_0, target, tail, lam_out):
        total = jnp.sum(got[...], 0)
        tail[...] = end[...] + total[:, 0:K] / (TAIL * total_rows)
        ret = total[:, K : 2 * K] / copies
        fresh = jnp.maximum(lam_old[...] + STEP_L * (target[...] - ret / total_cols), 0.0)
        lam_out[...] = (2.0 / 3.0) * (2.0 * fresh - lam_old[...]) + lam_0[...] / 3.0

    return call(
        body, "finished", (sums, t_out, lam, lam_start, goal), [shape(1, K)] * 2, nbytes=devices * 512
    )


def pinned(a):
    return pltpu.with_memory_space_constraint(a, pltpu.VMEM)


def across(values, axis):
    return lax.ppermute(values, axis, [(0, 1), (1, 0)])


def exchanged(payload, others):
    payload, others = lax.optimization_barrier((payload, others))
    received = lax.all_to_all(payload, SCEN, 0, 0)
    return lax.optimization_barrier((received, others))


def local(returns, mean_return, targets, weights, threshold, duals, multiplier):
    scen_rows, cols = returns.shape
    total_cols = cols * 4
    total_rows = scen_rows * 32
    width = scen_rows // 4
    mean_row = mean_return.reshape(1, cols)
    t0 = threshold.reshape(1, K)
    lam0 = multiplier.reshape(1, K)
    goal = targets.reshape(1, K)

    payload, returns, duals = first_gradient(duals, returns)
    returns = pinned(returns)
    held = (returns, duals, weights, mean_row, t0, lam0, goal)
    received, held = exchanged(payload, held)
    returns, duals, weights, mean_row, t0, lam0, goal = held
    own_first = own_rows(received, weights, t0, mean_row, True, total_cols, total_rows)
    gathered_first = lax.all_gather(own_first, ASSET)
    payload, lam0 = projected(
        gathered_first, own_first, gathered_first, own_first, lam0, goal, True, total_cols
    )
    held = (returns, duals, weights, mean_row, t0, lam0, goal, gathered_first, own_first)
    received, held = exchanged(payload, held)
    returns, duals, weights, mean_row, t0, lam0, goal, gathered_first, own_first = held
    returns = pinned(returns)
    v1, bars, t1, bar1, ret1 = unpacked(received, weights, weights, mean_row, t0, False)

    parts = []
    keep_tails = []
    take_tails = []
    for quarter in range(2):
        send, send_tail = loss_part(bars, returns, 0, lambda: quarter, width)
        take = across(send, "core")
        take_tails.append(across(send_tail, "core"))
        keep, keep_tail = loss_part(bars, returns, 1, lambda: quarter, width)
        keep_tails.append(keep_tail)
        parts.append(plus(keep, take))
    others = [across(part, "xh") for part in parts]
    send_tail, tail_a = own_and_other(keep_tails, take_tails)

    ua = dual_rows(parts[0], others[0], duals, bar1, 0, width)
    taken_a = across(ua, "core")
    sums = gradient_part([(ua, 1, 0)], returns, (), width)
    ub = dual_rows(parts[1], others[1], duals, bar1, 1, width)
    taken_b = across(ub, "core")
    sums = gradient_part([(taken_a, 0, 0), (ub, 1, 1)], returns, sums, width)
    payload = gradient_end(taken_b, 0, 1, returns, sums, width)
    tail_b = across(send_tail, "xh")

    held = (returns, duals, weights, mean_row, v1, t0, t1, lam0, goal, gathered_first, own_first)
    held = held + (ret1, ua, ub, tail_a, tail_b)
    received, held = exchanged(payload, held)
    returns, duals, weights, mean_row, v1, t0, t1, lam0, goal, gathered_first, own_first = held[:11]
    ret1, ua, ub, tail_a, tail_b = held[11:]
    own = own_rows(received, v1, t1, ret1, False, total_cols, total_rows)
    gathered = lax.all_gather(own, ASSET)
    payload, lam1 = projected(
        gathered, own, gathered_first, own_first, lam0, goal, False, total_cols
    )
    held = (returns, duals, weights, mean_row, v1, t0, t1, lam0, lam1, goal, ua, ub, tail_a, tail_b)
    received, held = exchanged(payload, held)
    returns, duals, weights, mean_row, v1, t0, t1, lam0, lam1, goal, ua, ub, tail_a, tail_b = held
    returns = pinned(returns)
    v2, bars, t2, bar2, ret2, weights_out = unpacked(received, v1, weights, mean_row, t1, True)

    def far_quarter():
        return 1 - lax.axis_index("xh")

    def own_quarter():
        return lax.axis_index("xh")

    parts = []
    for quarter in (far_quarter, own_quarter):
        (send,) = loss_part(bars, returns, 0, quarter, width)
        take = across(send, "core")
        (keep,) = loss_part(bars, returns, 1, quarter, width)
        parts.append(plus(keep, take))
    other = across(parts[0], "xh")

    quarter, t_out, sums = final_duals(
        parts[1], other, (tail_a, tail_b), (ua, ub), duals, t2, t1, t0, bar2, ret2, width
    )
    near = across(quarter, "xh")
    far = across(quarter, "core")
    far_near = across(near, "core")
    sums = lax.all_to_all(sums, ALL, 0, 0)
    duals_out = joined((far_near, near, far, quarter), width)
    tail_risk, lam_out = finished(sums, t_out, lam1, lam0, goal, total_cols, total_rows)
    return (weights_out, t_out.reshape(K), duals_out, lam_out.reshape(K), tail_risk.reshape(K))


def solution(mesh):
    split = Mesh(mesh.devices.reshape(4, 4, 2, 2, 2), ALL)
    in_specs = (P(SCEN, ASSET), P(ASSET), P(), P(None, ASSET), P(), P(None, SCEN), P())
    out_specs = (P(None, ASSET), P(), P(None, SCEN), P(), P())
    return jax.shard_map(local, mesh=split, in_specs=in_specs, out_specs=out_specs, check_vma=False)
```

```python
import math

import jax
import jax.numpy as jnp
from jax import lax
from jax.experimental import pallas as pl
from jax.experimental.pallas import tpu as pltpu
from jax.sharding import Mesh
from jax.sharding import PartitionSpec as P

BISECT = 6
TAIL = 0.2
STEP_V = 1.0
STEP_T = 0.5
STEP_U = 0.5
STEP_L = 2.0

SCEN = ("z", "y", "xl")
ASSET = ("xh", "core")
ALL = SCEN + ASSET

K = 64
HALF = 32
LANES = 128
TILE = 768

F32 = jnp.float32
BF16 = jnp.bfloat16

VMEM = pl.BlockSpec(memory_space=pltpu.VMEM)
SMEM = pl.BlockSpec(memory_space=pltpu.SMEM)
ANY = pl.BlockSpec(memory_space=pl.ANY)


def params():
    return pltpu.CompilerParams(vmem_limit_bytes=12 << 20)


def shape(*dims, dtype=F32):
    return jax.ShapeDtypeStruct(dims, dtype)


def cost(macs, nbytes):
    return pl.CostEstimate(flops=2 * macs // 100, bytes_accessed=nbytes // 100, transcendentals=0)


def start_of(offset):
    return pl.multiple_of(offset, LANES)


def lane_folded(values):
    total = values[:, 0:LANES]
    for j in range(1, values.shape[1] // LANES):
        total = total + values[:, j * LANES : (j + 1) * LANES]
    return total


def row_total(folded):
    return jnp.broadcast_to(jnp.sum(folded, 1, keepdims=True), folded.shape)


def diagonal(rows, first=0):
    return lax.broadcasted_iota(jnp.int32, (rows, LANES), 1) == first + lax.broadcasted_iota(
        jnp.int32, (rows, LANES), 0
    )


def in_lanes(column):
    return jnp.sum(jnp.where(diagonal(K), column, 0.0), 0, keepdims=True)[:, 0:K]


def in_rows(line):
    square = diagonal(K)[:, 0:K]
    return jnp.sum(jnp.where(square, jnp.broadcast_to(line, (K, K)), 0.0), 1, keepdims=True)


def picked(line, row):
    at = lax.broadcasted_iota(jnp.int32, line.shape, 1) == row
    return jnp.sum(jnp.where(at, line, 0.0), 1, keepdims=True)


def row_base(core_side, quarter, width):
    core = lax.axis_index("core")
    half = core if core_side else 1 - core
    return start_of((half * 2 + quarter) * width)


def scen_index():
    return (lax.axis_index("z") * 4 + lax.axis_index("y")) * 2 + lax.axis_index("xl")


def call(body, name, operands, outs, macs=0, nbytes=0, scratch=(), in_specs=None):
    single = not isinstance(outs, list)
    return pl.pallas_call(
        body,
        in_specs=in_specs or [VMEM] * len(operands),
        out_specs=VMEM if single else [VMEM] * len(outs),
        out_shape=outs,
        scratch_shapes=list(scratch),
        compiler_params=params(),
        cost_estimate=cost(macs, nbytes),
        name=name,
    )(*operands)


def pack(acc, out):
    blocks = acc.shape[1] // LANES
    for j in range(blocks):
        out[:, j, :] = acc[0:HALF, j * LANES : (j + 1) * LANES]
        out[:, blocks + j, :] = acc[HALF:K, j * LANES : (j + 1) * LANES]


def packed_shape(cols):
    return shape(HALF, 2 * cols // LANES, LANES)


def first_gradient(duals, returns):
    rows, cols = returns.shape
    steps = rows // TILE

    def body(u, r, out, mass, held, kept, acc, sems, dual_sems):
        copies = []
        for i in range(steps):
            at = pl.ds(i * TILE, TILE)
            mine = pltpu.make_async_copy(u.at[:, at], kept.at[:, at], dual_sems.at[i])
            block = pltpu.make_async_copy(r.at[at], held.at[at], sems.at[i])
            mine.start()
            block.start()
            copies.append((mine, block))
        folded = jnp.zeros((K, LANES), F32)
        for i in range(steps):
            copies[i][0].wait()
            part = kept[:, i * TILE : (i + 1) * TILE]
            folded = folded + lane_folded(part)
            copies[i][1].wait()
            term = jnp.dot(
                part.astype(BF16), held[pl.ds(i * TILE, TILE), :], preferred_element_type=F32
            )
            acc[...] = term if i == 0 else acc[...] + term
        pack(acc[...], out)
        mass[...] = in_lanes(row_total(folded))

    operands = [pltpu.with_memory_space_constraint(a, pltpu.HBM) for a in (duals, returns)]
    outs = [
        packed_shape(cols),
        shape(1, K),
        pltpu.VMEM((rows, cols), BF16),
        pltpu.VMEM((K, rows), F32),
    ]
    scratch = (
        pltpu.VMEM((K, cols), F32),
        pltpu.SemaphoreType.DMA((steps,)),
        pltpu.SemaphoreType.DMA((steps,)),
    )
    return call(
        body, "first_gradient", operands, outs, K * rows * cols, 2 * rows * cols, scratch, [ANY, ANY]
    )


def own_rows(received, state, extra, passed, first, total_cols, total_rows):
    scale = math.sqrt(total_cols / total_rows)
    cols = state.shape[1]
    blocks = cols // LANES
    lines = 2 * blocks

    def body(got, v, more, *refs):
        s = scen_index()
        grad = jnp.sum(got[...], 0)
        if first:
            out, line_out = refs
            for j in range(blocks):
                piece = more[pl.ds(j * LANES, LANES)].reshape(1, LANES)
                line_out[:, j * LANES : (j + 1) * LANES] = piece
                out[lines + j : lines + j + 1, :] = piece
                out[lines + blocks + j : lines + blocks + j + 1, :] = piece
        else:
            through, out, through_out = refs
            through_out[...] = through[...]
            out[lines:, :] = jnp.zeros((out.shape[0] - lines, LANES), F32)
            out[lines : lines + 1, 0:K] = more[...]
        for half in range(2):
            values = v[half * HALF : (half + 1) * HALF, :]
            at = lax.broadcasted_iota(jnp.int32, values.shape, 0) == s
            old = jnp.sum(jnp.where(at, values, 0.0), 0, keepdims=True)
            for j in range(blocks):
                line = half * blocks + j
                out[line : line + 1, :] = (
                    old[:, j * LANES : (j + 1) * LANES] + STEP_V * scale * grad[line : line + 1, :]
                )

    operands = (received, state, extra) + ((passed,) if passed is not None else ())
    outs = [shape(2 * lines, LANES), shape(1, cols)] if first else [shape(lines + 8, LANES)]
    if passed is not None:
        outs.append(shape(*passed.shape))
    return call(body, "own_rows", operands, outs, nbytes=4 * HALF * lines * LANES)


def projected(gathered, own, gathered_first, own_first, lam_old, goal, mass, first, total_cols):
    lines = gathered_first.shape[1] // 2
    blocks = lines // 2

    def body(rows, mine, means, mean, lam_in, target, sums_in, out, lam_out):
        s = scen_index()
        first_row = lax.broadcasted_iota(jnp.int32, (lines, LANES), 0) < blocks

        def sums(values):
            a = jnp.sum(jnp.where(first_row, values, 0.0), (0, 1), keepdims=True)
            b = jnp.sum(jnp.where(first_row, 0.0, values), (0, 1), keepdims=True)
            return jnp.concatenate([a, b], 0)

        def spread(pair):
            return jnp.where(first_row, pair[0:1, :], pair[1:2, :])

        lam = lam_in[...]
        if not first:
            ret = rows[0, lines : lines + 1, 0:K]
            for i in range(1, rows.shape[0]):
                ret = ret + rows[i, lines : lines + 1, 0:K]
            lam = jnp.maximum(lam + STEP_L * (target[...] - ret / total_cols), 0.0)
        lam_out[...] = lam
        slope = STEP_V * spread(jnp.concatenate([picked(lam, s), picked(lam, s + HALF)], 0))
        parts = [
            rows[i, 0:lines, :] + slope * means[i, lines : 2 * lines, :]
            for i in range(rows.shape[0])
        ]
        total = parts[0]
        top = parts[0]
        for part in parts[1:]:
            total = total + part
            top = jnp.maximum(top, part)
        low = jnp.min(top, (0, 1), keepdims=True)
        top_a = jnp.max(jnp.where(first_row, top, low), (0, 1), keepdims=True)
        top_b = jnp.max(jnp.where(first_row, low, top), (0, 1), keepdims=True)
        upper = jnp.concatenate([top_a, top_b], 0)
        lower = sums(total) / total_cols - 1.0

        def excess_at(level):
            wide = spread(level)
            over = jnp.maximum(parts[0] - wide, 0.0)
            for part in parts[1:]:
                over = over + jnp.maximum(part - wide, 0.0)
            return sums(over) - total_cols

        f_low = excess_at(lower)
        f_up = jnp.zeros_like(lower) - total_cols
        for _ in range(BISECT):
            middle = (lower + upper) * 0.5
            excess = excess_at(middle)
            raise_low = excess >= 0
            lower = jnp.where(raise_low, middle, lower)
            upper = jnp.where(raise_low, upper, middle)
            f_low = jnp.where(raise_low, excess, f_low)
            f_up = jnp.where(raise_low, f_up, excess)
        theta = lower + f_low * (upper - lower) / (f_low - f_up)
        x = mine[0:lines, :] + slope * mean[lines : 2 * lines, :]
        fresh = jnp.maximum(x - spread(theta), 0.0)
        mass = jnp.concatenate([sums_in[...], jnp.zeros((1, LANES - K), F32)], 1)
        rest = jnp.concatenate([mass, jnp.zeros((HALF - lines - 1, LANES), F32)], 0)
        for i in range(HALF):
            out[i, 0:lines, :] = fresh
            out[i, lines:HALF, :] = rest

    return call(
        body,
        "projected",
        (gathered, own, gathered_first, own_first, lam_old, goal, mass),
        [shape(HALF, HALF, LANES), shape(1, K)],
        nbytes=4 * HALF * HALF * LANES,
    )


def unpacked(received, state, start, mean_row, t_old, last, total_rows):
    cols = state.shape[1]
    blocks = cols // LANES

    def body(got, v, w, m, t, fresh, bars, t_new, t_bar, ret):
        for j in range(blocks):
            at = slice(j * LANES, (j + 1) * LANES)
            fresh[0:HALF, at] = got[:, j, :]
            fresh[HALF:K, at] = got[:, blocks + j, :]
        mass = jnp.sum(got[:, 2 * blocks, :], 0, keepdims=True)[:, 0:K]
        t_end = t[...] - STEP_T * (1.0 - mass / total_rows / TAIL)
        t_new[...] = t_end
        t_bar[...] = jnp.broadcast_to(in_rows(2.0 * t_end - t[...]), (K, LANES))
        bar = 2.0 * fresh[...] - v[...]
        bars[0:K, :] = (-bar).astype(BF16)
        if not last:
            bars[K : 2 * K, :] = (-w[...]).astype(BF16)
        ret[...] = in_lanes(row_total(lane_folded(bar * m[...])))

    outs = [
        shape(K, cols),
        shape((1 if last else 2) * K, cols, dtype=BF16),
        shape(1, K),
        shape(K, LANES),
        shape(1, K),
    ]
    return call(
        body, "unpacked", (received, state, start, mean_row, t_old), outs, nbytes=20 * K * cols
    )


def averaged(fresh, old, start):
    def body(new, v, w, out):
        out[...] = (2.0 / 3.0) * (2.0 * new[...] - v[...]) + w[...] / 3.0

    return call(body, "averaged", (fresh, old, start), shape(*start.shape), nbytes=16 * start.size)


def loss_part(bars, returns, sides, quarter, width):
    cols = returns.shape[1]
    count = bars.shape[0] // K

    def body(b, r, *outs):
        for index, side in enumerate(sides):
            base = row_base(side, quarter(), width)
            for i in range(width // TILE):
                at = slice(i * TILE, (i + 1) * TILE)
                block = r[pl.ds(start_of(base + i * TILE), TILE), :]
                term = lax.dot_general(
                    block, b[...], (((1,), (1,)), ((), ())), preferred_element_type=F32
                ).T
                for part in range(count):
                    outs[index * count + part][:, at] = term[part * K : (part + 1) * K, :]

    outs = [shape(K, width)] * (count * len(sides))
    return call(
        body,
        "loss_part",
        (bars, returns),
        outs,
        len(outs) * K * width * cols,
        2 * len(sides) * width * cols,
    )


def plus(a, b):
    def body(x, y, out):
        out[...] = x[...] + y[...]

    return call(body, "plus", (a, b), shape(*a.shape), nbytes=12 * a.size)


def own_and_other(keeps, takes):
    def body(k0, t0, k1, t1, send, keep):
        near = k0[...] + t0[...]
        far = k1[...] + t1[...]
        swap = lax.axis_index("xh") == 0
        send[...] = jnp.where(swap, far, near)
        keep[...] = jnp.where(swap, near, far)

    return call(
        body,
        "own_and_other",
        (keeps[0], takes[0], keeps[1], takes[1]),
        [shape(*keeps[0].shape)] * 2,
        nbytes=24 * keeps[0].size,
    )


def dual_step(loss, duals, t_bar):
    return jnp.clip(duals + STEP_U * (loss - t_bar[:, 0:1]), 0.0, 1.0)


def dual_rows(parts, others, duals, t_bar, width):
    def body(pa, pb, oa, ob, u, t, ua, ub):
        for quarter, (p, o, fresh) in enumerate(((pa, oa, ua), (pb, ob, ub))):
            base = row_base(1, quarter, width)
            fresh[...] = dual_step(p[...] + o[...], u[:, pl.ds(base, width)], t[...])

    return call(
        body,
        "dual_rows",
        (*parts, *others, duals, t_bar),
        [shape(K, width)] * 2,
        nbytes=32 * K * width,
    )


def gradient_part(terms, returns, before, width):
    cols = returns.shape[1]
    count = len(terms)

    def body(r, *refs):
        fed, rest = refs[:count], refs[count:]
        acc_out, folded_out = rest[-2:]
        total = rest[0][...] if before else None
        folds = rest[1][...] if before else None
        for (_, side, quarter), ref in zip(terms, fed):
            base = row_base(side, quarter, width)
            value = ref[...]
            term = jnp.dot(
                value.astype(BF16), r[pl.ds(base, width), :], preferred_element_type=F32
            )
            total = term if total is None else total + term
            fold = lane_folded(value)
            folds = fold if folds is None else folds + fold
        acc_out[...] = total
        folded_out[...] = folds

    operands = [returns] + [values for values, _, _ in terms] + list(before)
    return call(
        body,
        "gradient_part",
        operands,
        [shape(K, cols), shape(K, LANES)],
        count * K * width * cols,
        2 * count * width * cols,
    )


def gradient_end(taken, side, quarter, returns, before, width):
    cols = returns.shape[1]

    def body(r, got, acc_in, folded_in, out, mass):
        base = row_base(side, quarter, width)
        term = acc_in[...] + jnp.dot(
            got[...].astype(BF16), r[pl.ds(base, width), :], preferred_element_type=F32
        )
        pack(term, out)
        mass[...] = in_lanes(row_total(folded_in[...] + lane_folded(got[...])))

    return call(
        body,
        "gradient_end",
        (returns, taken, *before),
        [packed_shape(cols), shape(1, K)],
        K * width * cols,
        2 * width * cols,
    )


def final_duals(part, other, tails, held, start, t_new, t_old, t_start, t_bar, ret, width):
    devices = 128

    def body(p, o, la, lb, ua, ub, u0, tn, t, ts, tb, er, duals_out, t_out, sums):
        mine = lax.axis_index("xh")
        base = row_base(1, mine, width)
        loss = p[...] + o[...]
        old = jnp.where(mine == 0, ua[...], ub[...])
        fresh = dual_step(loss, old, tb[...])
        duals_out[...] = (2.0 / 3.0) * (2.0 * fresh - old) + u0[:, pl.ds(base, width)] / 3.0
        end = (2.0 / 3.0) * (2.0 * tn[...] - t[...]) + ts[...] / 3.0
        t_out[...] = end
        tail = (2.0 / 3.0) * loss + (la[...] + lb[...]) / 3.0
        over = jnp.maximum(tail - in_rows(end), 0.0)
        line = jnp.concatenate([in_lanes(row_total(lane_folded(over))), er[...]], 1)
        sums[...] = jnp.broadcast_to(line[None], (devices, 1, LANES))

    operands = (part, other, *tails, *held, start, t_new, t_old, t_start, t_bar, ret)
    return call(
        body,
        "final_duals",
        operands,
        [shape(K, width), shape(1, K), shape(devices, 1, LANES)],
        nbytes=24 * K * width,
    )


def joined(pieces, width):
    def body(far_near, near, far, own, out):
        mine = lax.axis_index("xh")
        out[:, pl.ds(row_base(0, 1 - mine, width), width)] = far_near[...]
        out[:, pl.ds(row_base(1, 1 - mine, width), width)] = near[...]
        out[:, pl.ds(row_base(0, mine, width), width)] = far[...]
        out[:, pl.ds(row_base(1, mine, width), width)] = own[...]

    return call(body, "joined", pieces, shape(K, 4 * width), nbytes=32 * K * width)


def finished(sums, t_out, lam, lam_start, goal, total_cols, total_rows):
    devices = sums.shape[0]
    copies = devices // 4

    def body(got, end, lam_old, lam_0, target, tail, lam_out):
        total = jnp.sum(got[...], 0)
        tail[...] = end[...] + total[:, 0:K] / (TAIL * total_rows)
        ret = total[:, K : 2 * K] / copies
        fresh = jnp.maximum(lam_old[...] + STEP_L * (target[...] - ret / total_cols), 0.0)
        lam_out[...] = (2.0 / 3.0) * (2.0 * fresh - lam_old[...]) + lam_0[...] / 3.0

    return call(
        body, "finished", (sums, t_out, lam, lam_start, goal), [shape(1, K)] * 2, nbytes=devices * 512
    )


def pinned(a):
    return pltpu.with_memory_space_constraint(a, pltpu.VMEM)


def across(values, axis):
    return lax.ppermute(values, axis, [(0, 1), (1, 0)])


def exchanged(payload, others):
    payload, others = lax.optimization_barrier((payload, others))
    received = lax.all_to_all(payload, SCEN, 0, 0)
    return lax.optimization_barrier((received, others))


def local(returns, mean_return, targets, weights, threshold, duals, multiplier):
    scen_rows, cols = returns.shape
    total_cols = cols * 4
    total_rows = scen_rows * 32
    width = scen_rows // 4
    t0 = threshold.reshape(1, K)
    lam0 = multiplier.reshape(1, K)
    goal = targets.reshape(1, K)

    payload, mass, returns, duals = first_gradient(duals, returns)
    returns = pinned(returns)
    held = (returns, duals, weights, mean_return, t0, lam0, goal, mass)
    received, held = exchanged(payload, held)
    returns, duals, weights, mean_return, t0, lam0, goal, mass = held
    own_first, mean_row = own_rows(
        received, weights, mean_return, None, True, total_cols, total_rows
    )
    gathered_first = lax.all_gather(own_first, ASSET)
    payload, lam0 = projected(
        gathered_first, own_first, gathered_first, own_first, lam0, goal, mass, True, total_cols
    )
    held = (returns, duals, weights, mean_row, t0, lam0, goal, gathered_first, own_first)
    received, held = exchanged(payload, held)
    returns, duals, weights, mean_row, t0, lam0, goal, gathered_first, own_first = held
    returns = pinned(returns)
    v1, bars, t1, bar1, ret1 = unpacked(
        received, weights, weights, mean_row, t0, False, total_rows
    )

    send, send_tail_a = loss_part(bars, returns, (0,), lambda: 0, width)
    take = across(send, "core")
    keep, keep_tail_a = loss_part(bars, returns, (1,), lambda: 0, width)
    part_a = plus(keep, take)
    take_tail_a = across(send_tail_a, "core")
    part_a, bars, take_tail_a = lax.optimization_barrier((part_a, bars, take_tail_a))
    send, send_tail_b, keep, keep_tail_b = loss_part(bars, returns, (0, 1), lambda: 1, width)
    part_b = plus(keep, across(send, "core"))
    take_tail_b = across(send_tail_b, "core")
    others = (across(part_a, "xh"), across(part_b, "xh"))
    send_tail, tail_a = own_and_other((keep_tail_a, keep_tail_b), (take_tail_a, take_tail_b))

    others, send_tail = lax.optimization_barrier((others, send_tail))
    ua, ub = dual_rows((part_a, part_b), others, duals, bar1, width)
    taken_a = across(ua, "core")
    taken_b = across(ub, "core")
    sums = gradient_part([(ua, 1, 0), (ub, 1, 1)], returns, (), width)
    sums = gradient_part([(taken_a, 0, 0)], returns, sums, width)
    payload, mass = gradient_end(taken_b, 0, 1, returns, sums, width)

    held = (returns, duals, weights, mean_row, v1, t0, t1, lam0, goal, gathered_first, own_first)
    held = held + (ret1, ua, ub, tail_a, send_tail, mass)
    received, held = exchanged(payload, held)
    returns, duals, weights, mean_row, v1, t0, t1, lam0, goal, gathered_first, own_first = held[:11]
    ret1, ua, ub, tail_a, send_tail, mass = held[11:]
    own, send_tail = own_rows(received, v1, ret1, send_tail, False, total_cols, total_rows)
    tail_b = across(send_tail, "xh")
    gathered = lax.all_gather(own, ASSET)
    payload, lam1 = projected(
        gathered, own, gathered_first, own_first, lam0, goal, mass, False, total_cols
    )
    held = (returns, duals, weights, mean_row, v1, t0, t1, lam0, lam1, goal, ua, ub, tail_a, tail_b)
    received, held = exchanged(payload, held)
    returns, duals, weights, mean_row, v1, t0, t1, lam0, lam1, goal, ua, ub, tail_a, tail_b = held
    returns = pinned(returns)
    v2, bars, t2, bar2, ret2 = unpacked(received, v1, weights, mean_row, t1, True, total_rows)

    def far_quarter():
        return 1 - lax.axis_index("xh")

    def own_quarter():
        return lax.axis_index("xh")

    (send,) = loss_part(bars, returns, (0,), far_quarter, width)
    take = across(send, "core")
    (keep,) = loss_part(bars, returns, (1,), far_quarter, width)
    part_a = plus(keep, take)
    part_a, bars, v2 = lax.optimization_barrier((part_a, bars, v2))
    send, keep = loss_part(bars, returns, (0, 1), own_quarter, width)
    part_b = plus(keep, across(send, "core"))
    parts = (part_a, part_b)
    other = across(parts[0], "xh")
    weights_out = averaged(v2, v1, weights)
    part, weights_out = lax.optimization_barrier((parts[1], weights_out))

    quarter, t_out, sums = final_duals(
        part, other, (tail_a, tail_b), (ua, ub), duals, t2, t1, t0, bar2, ret2, width
    )
    near = across(quarter, "xh")
    far = across(quarter, "core")
    sums = lax.all_to_all(sums, ALL, 0, 0)
    near, far, sums = lax.optimization_barrier((near, far, sums))
    far_near = across(near, "core")
    duals_out = joined((far_near, near, far, quarter), width)
    sums, duals_out = lax.optimization_barrier((sums, duals_out))
    tail_risk, lam_out = finished(sums, t_out, lam1, lam0, goal, total_cols, total_rows)
    return (weights_out, t_out.reshape(K), duals_out, lam_out.reshape(K), tail_risk.reshape(K))


def solution(mesh):
    split = Mesh(mesh.devices.reshape(4, 4, 2, 2, 2), ALL)
    in_specs = (P(SCEN, ASSET), P(ASSET), P(), P(None, ASSET), P(), P(None, SCEN), P())
    out_specs = (P(None, ASSET), P(), P(None, SCEN), P(), P())
    return jax.shard_map(local, mesh=split, in_specs=in_specs, out_specs=out_specs, check_vma=False)
```

```python
import math

import jax
import jax.numpy as jnp
from jax import lax
from jax.experimental import pallas as pl
from jax.experimental.pallas import tpu as pltpu
from jax.sharding import Mesh
from jax.sharding import PartitionSpec as P

BISECT = 6
TAIL = 0.2
STEP_V = 1.0
STEP_T = 0.5
STEP_U = 0.5
STEP_L = 2.0

SCEN = ("z", "y", "xl")
ASSET = ("xh", "core")
ALL = SCEN + ASSET

K = 64
HALF = 32
LANES = 128
TILE = 768

F32 = jnp.float32
BF16 = jnp.bfloat16

VMEM = pl.BlockSpec(memory_space=pltpu.VMEM)
SMEM = pl.BlockSpec(memory_space=pltpu.SMEM)
ANY = pl.BlockSpec(memory_space=pl.ANY)


def params():
    return pltpu.CompilerParams(vmem_limit_bytes=12 << 20)


def shape(*dims, dtype=F32):
    return jax.ShapeDtypeStruct(dims, dtype)


def cost(macs, nbytes):
    return pl.CostEstimate(flops=2 * macs // 100, bytes_accessed=nbytes // 100, transcendentals=0)


def start_of(offset):
    return pl.multiple_of(offset, LANES)


def lane_folded(values):
    total = values[:, 0:LANES]
    for j in range(1, values.shape[1] // LANES):
        total = total + values[:, j * LANES : (j + 1) * LANES]
    return total


def row_total(folded):
    return jnp.broadcast_to(jnp.sum(folded, 1, keepdims=True), folded.shape)


def diagonal(rows, first=0):
    return lax.broadcasted_iota(jnp.int32, (rows, LANES), 1) == first + lax.broadcasted_iota(
        jnp.int32, (rows, LANES), 0
    )


def in_lanes(column):
    return jnp.sum(jnp.where(diagonal(K), column, 0.0), 0, keepdims=True)[:, 0:K]


def in_rows(line):
    square = diagonal(K)[:, 0:K]
    return jnp.sum(jnp.where(square, jnp.broadcast_to(line, (K, K)), 0.0), 1, keepdims=True)


def picked(line, row):
    at = lax.broadcasted_iota(jnp.int32, line.shape, 1) == row
    return jnp.sum(jnp.where(at, line, 0.0), 1, keepdims=True)


def row_base(core_side, quarter, width):
    core = lax.axis_index("core")
    half = core if core_side else 1 - core
    return start_of((half * 2 + quarter) * width)


def scen_index():
    return (lax.axis_index("z") * 4 + lax.axis_index("y")) * 2 + lax.axis_index("xl")


def call(
    body, name, operands, outs, macs=0, nbytes=0, scratch=(), in_specs=None, out_specs=None, aliases=None
):
    single = not isinstance(outs, list)
    return pl.pallas_call(
        body,
        in_specs=in_specs or [VMEM] * len(operands),
        out_specs=out_specs or (VMEM if single else [VMEM] * len(outs)),
        input_output_aliases=aliases or {},
        out_shape=outs,
        scratch_shapes=list(scratch),
        compiler_params=params(),
        cost_estimate=cost(macs, nbytes),
        name=name,
    )(*operands)


def pack(acc, out):
    blocks = acc.shape[1] // LANES
    for j in range(blocks):
        out[:, j, :] = acc[0:HALF, j * LANES : (j + 1) * LANES]
        out[:, blocks + j, :] = acc[HALF:K, j * LANES : (j + 1) * LANES]


def packed_shape(cols):
    return shape(HALF, 2 * cols // LANES, LANES)


def first_gradient(duals, returns):
    rows, cols = returns.shape
    steps = rows // TILE

    def body(u, r, out, mass, held, kept, acc, sems, dual_sems):
        copies = []
        for i in range(steps):
            at = pl.ds(i * TILE, TILE)
            mine = pltpu.make_async_copy(u.at[:, at], kept.at[:, at], dual_sems.at[i])
            block = pltpu.make_async_copy(r.at[at], held.at[at], sems.at[i])
            mine.start()
            block.start()
            copies.append((mine, block))
        folded = jnp.zeros((K, LANES), F32)
        for i in range(steps):
            copies[i][0].wait()
            part = kept[:, i * TILE : (i + 1) * TILE]
            folded = folded + lane_folded(part)
            copies[i][1].wait()
            term = jnp.dot(
                part.astype(BF16), held[pl.ds(i * TILE, TILE), :], preferred_element_type=F32
            )
            acc[...] = term if i == 0 else acc[...] + term
        pack(acc[...], out)
        mass[...] = in_lanes(row_total(folded))

    operands = [pltpu.with_memory_space_constraint(a, pltpu.HBM) for a in (duals, returns)]
    outs = [
        packed_shape(cols),
        shape(1, K),
        pltpu.VMEM((rows, cols), BF16),
        pltpu.VMEM((K, rows), F32),
    ]
    scratch = (
        pltpu.VMEM((K, cols), F32),
        pltpu.SemaphoreType.DMA((steps,)),
        pltpu.SemaphoreType.DMA((steps,)),
    )
    return call(
        body, "first_gradient", operands, outs, K * rows * cols, 2 * rows * cols, scratch, [ANY, ANY]
    )


def own_rows(received, state, extra, passed, first, total_cols, total_rows):
    scale = math.sqrt(total_cols / total_rows)
    cols = state.shape[1]
    blocks = cols // LANES
    lines = 2 * blocks

    def body(got, v, more, *refs):
        s = scen_index()
        grad = jnp.sum(got[...], 0)
        if first:
            out, line_out = refs
            for j in range(blocks):
                piece = more[pl.ds(j * LANES, LANES)].reshape(1, LANES)
                line_out[:, j * LANES : (j + 1) * LANES] = piece
                out[lines + j : lines + j + 1, :] = piece
                out[lines + blocks + j : lines + blocks + j + 1, :] = piece
        else:
            through, out, through_out = refs
            through_out[...] = through[...]
            out[lines:, :] = jnp.zeros((out.shape[0] - lines, LANES), F32)
            out[lines : lines + 1, 0:K] = more[...]
        for half in range(2):
            values = v[half * HALF : (half + 1) * HALF, :]
            at = lax.broadcasted_iota(jnp.int32, values.shape, 0) == s
            old = jnp.sum(jnp.where(at, values, 0.0), 0, keepdims=True)
            for j in range(blocks):
                line = half * blocks + j
                out[line : line + 1, :] = (
                    old[:, j * LANES : (j + 1) * LANES] + STEP_V * scale * grad[line : line + 1, :]
                )

    operands = (received, state, extra) + ((passed,) if passed is not None else ())
    outs = [shape(2 * lines, LANES), shape(1, cols)] if first else [shape(lines + 8, LANES)]
    if passed is not None:
        outs.append(shape(*passed.shape))
    return call(body, "own_rows", operands, outs, nbytes=4 * HALF * lines * LANES)


def projected(gathered, own, gathered_first, own_first, lam_old, goal, mass, first, total_cols):
    lines = gathered_first.shape[1] // 2
    blocks = lines // 2

    def body(rows, mine, means, mean, lam_in, target, sums_in, out, lam_out):
        s = scen_index()
        first_row = lax.broadcasted_iota(jnp.int32, (lines, LANES), 0) < blocks

        def sums(values):
            a = jnp.sum(jnp.where(first_row, values, 0.0), (0, 1), keepdims=True)
            b = jnp.sum(jnp.where(first_row, 0.0, values), (0, 1), keepdims=True)
            return jnp.concatenate([a, b], 0)

        def spread(pair):
            return jnp.where(first_row, pair[0:1, :], pair[1:2, :])

        lam = lam_in[...]
        if not first:
            ret = rows[0, lines : lines + 1, 0:K]
            for i in range(1, rows.shape[0]):
                ret = ret + rows[i, lines : lines + 1, 0:K]
            lam = jnp.maximum(lam + STEP_L * (target[...] - ret / total_cols), 0.0)
        lam_out[...] = lam
        slope = STEP_V * spread(jnp.concatenate([picked(lam, s), picked(lam, s + HALF)], 0))
        parts = [
            rows[i, 0:lines, :] + slope * means[i, lines : 2 * lines, :]
            for i in range(rows.shape[0])
        ]
        total = parts[0]
        top = parts[0]
        for part in parts[1:]:
            total = total + part
            top = jnp.maximum(top, part)
        low = jnp.min(top, (0, 1), keepdims=True)
        top_a = jnp.max(jnp.where(first_row, top, low), (0, 1), keepdims=True)
        top_b = jnp.max(jnp.where(first_row, low, top), (0, 1), keepdims=True)
        upper = jnp.concatenate([top_a, top_b], 0)
        lower = sums(total) / total_cols - 1.0

        def excess_at(level):
            wide = spread(level)
            over = jnp.maximum(parts[0] - wide, 0.0)
            for part in parts[1:]:
                over = over + jnp.maximum(part - wide, 0.0)
            return sums(over) - total_cols

        f_low = excess_at(lower)
        f_up = jnp.zeros_like(lower) - total_cols
        for _ in range(BISECT):
            middle = (lower + upper) * 0.5
            excess = excess_at(middle)
            raise_low = excess >= 0
            lower = jnp.where(raise_low, middle, lower)
            upper = jnp.where(raise_low, upper, middle)
            f_low = jnp.where(raise_low, excess, f_low)
            f_up = jnp.where(raise_low, f_up, excess)
        theta = lower + f_low * (upper - lower) / (f_low - f_up)
        x = mine[0:lines, :] + slope * mean[lines : 2 * lines, :]
        fresh = jnp.maximum(x - spread(theta), 0.0)
        mass = jnp.concatenate([sums_in[...], jnp.zeros((1, LANES - K), F32)], 1)
        for i in range(HALF):
            for half in range(2):
                out[i, 0:blocks, half, :] = fresh[half * blocks : (half + 1) * blocks, :]
                out[i, blocks : blocks + 1, half, :] = mass

    return call(
        body,
        "projected",
        (gathered, own, gathered_first, own_first, lam_old, goal, mass),
        [shape(HALF, blocks + 1, 2, LANES), shape(1, K)],
        nbytes=4 * HALF * HALF * LANES,
    )


def unpacked(received, state, start, mean_row, t_old, last, total_rows):
    cols = state.shape[1]
    blocks = cols // LANES

    def body(got, v, w, m, t, fresh, bars, t_new, t_bar, ret):
        for j in range(blocks):
            at = slice(j * LANES, (j + 1) * LANES)
            fresh[0:HALF, at] = got[:, j, 0, :]
            fresh[HALF:K, at] = got[:, j, 1, :]
        mass = jnp.sum(got[:, blocks, 0, :], 0, keepdims=True)[:, 0:K]
        t_end = t[...] - STEP_T * (1.0 - mass / total_rows / TAIL)
        t_new[...] = t_end
        t_bar[...] = jnp.broadcast_to(in_rows(2.0 * t_end - t[...]), (K, LANES))
        bar = 2.0 * fresh[...] - v[...]
        bars[0:K, :] = (-bar).astype(BF16)
        if not last:
            bars[K : 2 * K, :] = (-w[...]).astype(BF16)
        ret[...] = in_lanes(row_total(lane_folded(bar * m[...])))

    outs = [
        shape(K, cols),
        shape((1 if last else 2) * K, cols, dtype=BF16),
        shape(1, K),
        shape(K, LANES),
        shape(1, K),
    ]
    return call(
        body, "unpacked", (received, state, start, mean_row, t_old), outs, nbytes=20 * K * cols
    )


def averaged(fresh, old, start):
    def body(new, v, w, out):
        out[...] = (2.0 / 3.0) * (2.0 * new[...] - v[...]) + w[...] / 3.0

    return call(body, "averaged", (fresh, old, start), shape(*start.shape), nbytes=16 * start.size)


def loss_part(bars, returns, sides, quarter, width):
    cols = returns.shape[1]
    count = bars.shape[0] // K

    def body(b, r, *outs):
        for index, side in enumerate(sides):
            base = row_base(side, quarter(), width)
            for i in range(width // TILE):
                at = slice(i * TILE, (i + 1) * TILE)
                block = r[pl.ds(start_of(base + i * TILE), TILE), :]
                term = lax.dot_general(
                    block, b[...], (((1,), (1,)), ((), ())), preferred_element_type=F32
                ).T
                for part in range(count):
                    outs[index * count + part][:, at] = term[part * K : (part + 1) * K, :]

    outs = [shape(K, width)] * (count * len(sides))
    return call(
        body,
        "loss_part",
        (bars, returns),
        outs,
        len(outs) * K * width * cols,
        2 * len(sides) * width * cols,
    )


def plus(a, b):
    def body(x, y, out):
        out[...] = x[...] + y[...]

    return call(body, "plus", (a, b), shape(*a.shape), nbytes=12 * a.size)


def own_and_other(keeps, takes):
    def body(k0, t0, k1, t1, send, keep):
        near = k0[...] + t0[...]
        far = k1[...] + t1[...]
        swap = lax.axis_index("xh") == 0
        send[...] = jnp.where(swap, far, near)
        keep[...] = jnp.where(swap, near, far)

    return call(
        body,
        "own_and_other",
        (keeps[0], takes[0], keeps[1], takes[1]),
        [shape(*keeps[0].shape)] * 2,
        nbytes=24 * keeps[0].size,
    )


def dual_step(loss, duals, t_bar):
    return jnp.clip(duals + STEP_U * (loss - t_bar[:, 0:1]), 0.0, 1.0)


def dual_row(part, other, duals, t_bar, quarter, width):
    def body(p, o, u, t, fresh):
        base = row_base(1, quarter, width)
        fresh[...] = dual_step(p[...] + o[...], u[:, pl.ds(base, width)], t[...])

    return call(body, "dual_row", (part, other, duals, t_bar), shape(K, width), nbytes=16 * K * width)


def gradient_part(terms, returns, before, width):
    cols = returns.shape[1]
    count = len(terms)

    def body(r, *refs):
        fed, rest = refs[:count], refs[count:]
        acc_out, folded_out = rest[-2:]
        total = rest[0][...] if before else None
        folds = rest[1][...] if before else None
        for (_, side, quarter), ref in zip(terms, fed):
            base = row_base(side, quarter, width)
            value = ref[...]
            term = jnp.dot(
                value.astype(BF16), r[pl.ds(base, width), :], preferred_element_type=F32
            )
            total = term if total is None else total + term
            fold = lane_folded(value)
            folds = fold if folds is None else folds + fold
        acc_out[...] = total
        folded_out[...] = folds

    operands = [returns] + [values for values, _, _ in terms] + list(before)
    return call(
        body,
        "gradient_part",
        operands,
        [shape(K, cols), shape(K, LANES)],
        count * K * width * cols,
        2 * count * width * cols,
    )


def gradient_end(taken, side, quarter, returns, before, width):
    cols = returns.shape[1]

    def body(r, got, acc_in, folded_in, out, mass):
        base = row_base(side, quarter, width)
        term = acc_in[...] + jnp.dot(
            got[...].astype(BF16), r[pl.ds(base, width), :], preferred_element_type=F32
        )
        pack(term, out)
        mass[...] = in_lanes(row_total(folded_in[...] + lane_folded(got[...])))

    return call(
        body,
        "gradient_end",
        (returns, taken, *before),
        [packed_shape(cols), shape(1, K)],
        K * width * cols,
        2 * width * cols,
    )


def final_duals(part, other, tails, held, start, t_new, t_old, t_start, t_bar, ret, width):
    devices = 128

    def body(p, o, la, lb, ua, ub, u0, tn, t, ts, tb, er, duals_out, t_out, sums):
        mine = lax.axis_index("xh")
        base = row_base(1, mine, width)
        loss = p[...] + o[...]
        old = jnp.where(mine == 0, ua[...], ub[...])
        fresh = dual_step(loss, old, tb[...])
        duals_out[...] = (2.0 / 3.0) * (2.0 * fresh - old) + u0[:, pl.ds(base, width)] / 3.0
        end = (2.0 / 3.0) * (2.0 * tn[...] - t[...]) + ts[...] / 3.0
        t_out[...] = end
        tail = (2.0 / 3.0) * loss + (la[...] + lb[...]) / 3.0
        over = jnp.maximum(tail - in_rows(end), 0.0)
        line = jnp.concatenate([in_lanes(row_total(lane_folded(over))), er[...]], 1)
        sums[...] = jnp.broadcast_to(line[None], (devices, 1, LANES))

    operands = (part, other, *tails, *held, start, t_new, t_old, t_start, t_bar, ret)
    return call(
        body,
        "final_duals",
        operands,
        [shape(K, width), shape(1, K), shape(devices, 1, LANES)],
        nbytes=24 * K * width,
    )


def joined(pieces, width):
    def body(near, far, own, out, sems):
        mine = lax.axis_index("xh")
        places = ((1, 1 - mine, near), (0, mine, far), (1, mine, own))
        copies = []
        for i, (side, quarter, ref) in enumerate(places):
            to = out.at[:, pl.ds(row_base(side, quarter, width), width)]
            copies.append(pltpu.make_async_copy(ref, to, sems.at[i]))
        for copy in copies:
            copy.start()
        for copy in copies:
            copy.wait()

    return call(
        body,
        "joined",
        pieces,
        pltpu.HBM((K, 4 * width), F32),
        nbytes=24 * K * width,
        scratch=(pltpu.SemaphoreType.DMA((3,)),),
        out_specs=ANY,
    )


def completed(duals_out, last, width):
    def body(before, piece, out, sem):
        to = out.at[:, pl.ds(row_base(0, 1 - lax.axis_index("xh"), width), width)]
        copy = pltpu.make_async_copy(piece, to, sem)
        copy.start()
        copy.wait()

    return call(
        body,
        "completed",
        (duals_out, last),
        pltpu.HBM(duals_out.shape, F32),
        nbytes=8 * K * width,
        scratch=(pltpu.SemaphoreType.DMA,),
        in_specs=[ANY, VMEM],
        out_specs=ANY,
        aliases={0: 0},
    )


def finished(sums, t_out, lam, lam_start, goal, total_cols, total_rows):
    devices = sums.shape[0]
    copies = devices // 4

    def body(got, end, lam_old, lam_0, target, tail, lam_out):
        total = jnp.sum(got[...], 0)
        tail[...] = end[...] + total[:, 0:K] / (TAIL * total_rows)
        ret = total[:, K : 2 * K] / copies
        fresh = jnp.maximum(lam_old[...] + STEP_L * (target[...] - ret / total_cols), 0.0)
        lam_out[...] = (2.0 / 3.0) * (2.0 * fresh - lam_old[...]) + lam_0[...] / 3.0

    return call(
        body, "finished", (sums, t_out, lam, lam_start, goal), [shape(1, K)] * 2, nbytes=devices * 512
    )


def pinned(a):
    return pltpu.with_memory_space_constraint(a, pltpu.VMEM)


def across(values, axis):
    return lax.ppermute(values, axis, [(0, 1), (1, 0)])


def plus_gathered(a, both):
    def body(x, y, out):
        core = lax.axis_index("core")
        out[...] = x[...] + y[1 - core]

    return call(body, "plus", (a, both), shape(*a.shape), nbytes=12 * a.size)


def exchanged(payload, others):
    payload, others = lax.optimization_barrier((payload, others))
    received = lax.all_to_all(payload, SCEN, 0, 0)
    return lax.optimization_barrier((received, others))


def local(returns, mean_return, targets, weights, threshold, duals, multiplier):
    scen_rows, cols = returns.shape
    total_cols = cols * 4
    total_rows = scen_rows * 32
    width = scen_rows // 4
    t0 = threshold.reshape(1, K)
    lam0 = multiplier.reshape(1, K)
    goal = targets.reshape(1, K)

    payload, mass, returns, duals = first_gradient(duals, returns)
    returns = pinned(returns)
    held = (returns, duals, weights, mean_return, t0, lam0, goal, mass)
    received, held = exchanged(payload, held)
    returns, duals, weights, mean_return, t0, lam0, goal, mass = held
    own_first, mean_row = own_rows(
        received, weights, mean_return, None, True, total_cols, total_rows
    )
    gathered_first = lax.all_gather(own_first, ASSET)
    payload, lam0 = projected(
        gathered_first, own_first, gathered_first, own_first, lam0, goal, mass, True, total_cols
    )
    held = (returns, duals, weights, mean_row, t0, lam0, goal, gathered_first, own_first)
    received, held = exchanged(payload, held)
    returns, duals, weights, mean_row, t0, lam0, goal, gathered_first, own_first = held
    returns = pinned(returns)
    v1, bars, t1, bar1, ret1 = unpacked(
        received, weights, weights, mean_row, t0, False, total_rows
    )

    send, send_tail_a = loss_part(bars, returns, (0,), lambda: 0, width)
    take = across(send, "core")
    keep, keep_tail_a = loss_part(bars, returns, (1,), lambda: 0, width)
    part_a = plus(keep, take)
    take_tail_a = across(send_tail_a, "core")
    part_a, bars, take_tail_a = lax.optimization_barrier((part_a, bars, take_tail_a))
    send, send_tail_b, keep, keep_tail_b = loss_part(bars, returns, (0, 1), lambda: 1, width)
    part_b = plus_gathered(keep, lax.all_gather(send, "core"))
    take_tail_b = across(send_tail_b, "core")
    others = (across(part_a, "xh"), across(part_b, "xh"))
    send_tail, tail_a = own_and_other((keep_tail_a, keep_tail_b), (take_tail_a, take_tail_b))

    ua = dual_row(part_a, others[0], duals, bar1, 0, width)
    taken_a = across(ua, "core")
    ub = dual_row(part_b, others[1], duals, bar1, 1, width)
    ub, send_tail = lax.optimization_barrier((ub, send_tail))
    taken_b = across(ub, "core")
    sums = gradient_part([(ua, 1, 0), (ub, 1, 1)], returns, (), width)
    sums = gradient_part([(taken_a, 0, 0)], returns, sums, width)
    payload, mass = gradient_end(taken_b, 0, 1, returns, sums, width)

    held = (returns, duals, weights, mean_row, v1, t0, t1, lam0, goal, gathered_first, own_first)
    held = held + (ret1, ua, ub, tail_a, send_tail, mass)
    received, held = exchanged(payload, held)
    returns, duals, weights, mean_row, v1, t0, t1, lam0, goal, gathered_first, own_first = held[:11]
    ret1, ua, ub, tail_a, send_tail, mass = held[11:]
    own, send_tail = own_rows(received, v1, ret1, send_tail, False, total_cols, total_rows)
    tail_b = across(send_tail, "xh")
    gathered = lax.all_gather(own, ASSET)
    payload, lam1 = projected(
        gathered, own, gathered_first, own_first, lam0, goal, mass, False, total_cols
    )
    held = (returns, duals, weights, mean_row, v1, t0, t1, lam0, lam1, goal, ua, ub, tail_a, tail_b)
    received, held = exchanged(payload, held)
    returns, duals, weights, mean_row, v1, t0, t1, lam0, lam1, goal, ua, ub, tail_a, tail_b = held
    returns = pinned(returns)
    v2, bars, t2, bar2, ret2 = unpacked(received, v1, weights, mean_row, t1, True, total_rows)

    def far_quarter():
        return 1 - lax.axis_index("xh")

    def own_quarter():
        return lax.axis_index("xh")

    (send,) = loss_part(bars, returns, (0,), far_quarter, width)
    take = across(send, "core")
    (keep,) = loss_part(bars, returns, (1,), far_quarter, width)
    part_a = plus(keep, take)
    part_a, bars, v2 = lax.optimization_barrier((part_a, bars, v2))
    send, keep = loss_part(bars, returns, (0, 1), own_quarter, width)
    part_b = plus_gathered(keep, lax.all_gather(send, "core"))
    parts = (part_a, part_b)
    other = across(parts[0], "xh")
    weights_out = averaged(v2, v1, weights)
    part, weights_out = lax.optimization_barrier((parts[1], weights_out))

    quarter, t_out, sums = final_duals(
        part, other, (tail_a, tail_b), (ua, ub), duals, t2, t1, t0, bar2, ret2, width
    )
    near = across(quarter, "xh")
    far = across(quarter, "core")
    sums = lax.all_to_all(sums, ALL, 0, 0)
    near, far, sums = lax.optimization_barrier((near, far, sums))
    far_near = across(near, "core")
    duals_out = completed(joined((near, far, quarter), width), far_near, width)
    tail_risk, lam_out = finished(sums, t_out, lam1, lam0, goal, total_cols, total_rows)
    return (weights_out, t_out.reshape(K), duals_out, lam_out.reshape(K), tail_risk.reshape(K))


def solution(mesh):
    split = Mesh(mesh.devices.reshape(4, 4, 2, 2, 2), ALL)
    in_specs = (P(SCEN, ASSET), P(ASSET), P(), P(None, ASSET), P(), P(None, SCEN), P())
    out_specs = (P(None, ASSET), P(), P(None, SCEN), P(), P())
    return jax.shard_map(local, mesh=split, in_specs=in_specs, out_specs=out_specs, check_vma=False)
```

```python
import math

import jax
import jax.numpy as jnp
from jax import lax
from jax.experimental import pallas as pl
from jax.experimental.pallas import tpu as pltpu
from jax.sharding import Mesh
from jax.sharding import PartitionSpec as P

BISECT = 6
AHEAD = 3
TAIL = 0.2
STEP_V = 1.0
STEP_T = 0.5
STEP_U = 0.5
STEP_L = 2.0

SCEN = ("z", "y", "xl")
ASSET = ("xh", "core")
ALL = SCEN + ASSET

K = 64
HALF = 32
LANES = 128
TILE = 768

F32 = jnp.float32
BF16 = jnp.bfloat16

VMEM = pl.BlockSpec(memory_space=pltpu.VMEM)
SMEM = pl.BlockSpec(memory_space=pltpu.SMEM)
ANY = pl.BlockSpec(memory_space=pl.ANY)


def params():
    return pltpu.CompilerParams(vmem_limit_bytes=12 << 20)


def shape(*dims, dtype=F32):
    return jax.ShapeDtypeStruct(dims, dtype)


def cost(macs, nbytes):
    return pl.CostEstimate(flops=2 * macs // 100, bytes_accessed=nbytes // 100, transcendentals=0)


def start_of(offset):
    return pl.multiple_of(offset, LANES)


def lane_folded(values):
    total = values[:, 0:LANES]
    for j in range(1, values.shape[1] // LANES):
        total = total + values[:, j * LANES : (j + 1) * LANES]
    return total


def row_total(folded):
    return jnp.broadcast_to(jnp.sum(folded, 1, keepdims=True), folded.shape)


def diagonal(rows, first=0):
    return lax.broadcasted_iota(jnp.int32, (rows, LANES), 1) == first + lax.broadcasted_iota(
        jnp.int32, (rows, LANES), 0
    )


def in_lanes(column):
    return jnp.sum(jnp.where(diagonal(K), column, 0.0), 0, keepdims=True)[:, 0:K]


def in_rows(line):
    square = diagonal(K)[:, 0:K]
    return jnp.sum(jnp.where(square, jnp.broadcast_to(line, (K, K)), 0.0), 1, keepdims=True)


def picked(line, row):
    at = lax.broadcasted_iota(jnp.int32, line.shape, 1) == row
    return jnp.sum(jnp.where(at, line, 0.0), 1, keepdims=True)


def row_base(core_side, quarter, width):
    core = lax.axis_index("core")
    half = core if core_side else 1 - core
    return start_of((half * 2 + quarter) * width)


def scen_index():
    return (lax.axis_index("z") * 4 + lax.axis_index("y")) * 2 + lax.axis_index("xl")


def call(
    body, name, operands, outs, macs=0, nbytes=0, scratch=(), in_specs=None, out_specs=None, aliases=None
):
    single = not isinstance(outs, list)
    return pl.pallas_call(
        body,
        in_specs=in_specs or [VMEM] * len(operands),
        out_specs=out_specs or (VMEM if single else [VMEM] * len(outs)),
        input_output_aliases=aliases or {},
        out_shape=outs,
        scratch_shapes=list(scratch),
        compiler_params=params(),
        cost_estimate=cost(macs, nbytes),
        name=name,
    )(*operands)


def pack(acc, out):
    blocks = acc.shape[1] // LANES
    for j in range(blocks):
        out[:, j, :] = acc[0:HALF, j * LANES : (j + 1) * LANES]
        out[:, blocks + j, :] = acc[HALF:K, j * LANES : (j + 1) * LANES]


def packed_shape(cols):
    return shape(HALF, 2 * cols // LANES, LANES)


def first_gradient(duals, returns):
    rows, cols = returns.shape
    steps = rows // TILE

    def body(u, r, out, mass, held, kept, acc, sems, dual_sems):
        copies = []
        for i in range(steps):
            at = pl.ds(i * TILE, TILE)
            mine = pltpu.make_async_copy(u.at[:, at], kept.at[:, at], dual_sems.at[i])
            block = pltpu.make_async_copy(r.at[at], held.at[at], sems.at[i])
            mine.start()
            block.start()
            copies.append((mine, block))
        folded = jnp.zeros((K, LANES), F32)
        for i in range(steps):
            copies[i][0].wait()
            part = kept[:, i * TILE : (i + 1) * TILE]
            folded = folded + lane_folded(part)
            copies[i][1].wait()
            term = jnp.dot(
                part.astype(BF16), held[pl.ds(i * TILE, TILE), :], preferred_element_type=F32
            )
            acc[...] = term if i == 0 else acc[...] + term
        pack(acc[...], out)
        mass[...] = in_lanes(row_total(folded))

    operands = [pltpu.with_memory_space_constraint(a, pltpu.HBM) for a in (duals, returns)]
    outs = [
        packed_shape(cols),
        shape(1, K),
        pltpu.VMEM((rows, cols), BF16),
        pltpu.VMEM((K, rows), F32),
    ]
    scratch = (
        pltpu.VMEM((K, cols), F32),
        pltpu.SemaphoreType.DMA((steps,)),
        pltpu.SemaphoreType.DMA((steps,)),
    )
    return call(
        body, "first_gradient", operands, outs, K * rows * cols, 2 * rows * cols, scratch, [ANY, ANY]
    )


def own_rows(received, state, extra, passed, first, total_cols, total_rows):
    scale = math.sqrt(total_cols / total_rows)
    cols = state.shape[1]
    blocks = cols // LANES
    lines = 2 * blocks

    def body(got, v, more, *refs):
        s = scen_index()
        grad = jnp.sum(got[...], 0)
        if first:
            out, line_out = refs
            for j in range(blocks):
                piece = more[pl.ds(j * LANES, LANES)].reshape(1, LANES)
                line_out[:, j * LANES : (j + 1) * LANES] = piece
                out[lines + j : lines + j + 1, :] = piece
                out[lines + blocks + j : lines + blocks + j + 1, :] = piece
        else:
            through, out, through_out = refs
            through_out[...] = through[...]
            out[lines:, :] = jnp.zeros((out.shape[0] - lines, LANES), F32)
            out[lines : lines + 1, 0:K] = more[...]
        for half in range(2):
            values = v[half * HALF : (half + 1) * HALF, :]
            at = lax.broadcasted_iota(jnp.int32, values.shape, 0) == s
            old = jnp.sum(jnp.where(at, values, 0.0), 0, keepdims=True)
            for j in range(blocks):
                line = half * blocks + j
                out[line : line + 1, :] = (
                    old[:, j * LANES : (j + 1) * LANES] + STEP_V * scale * grad[line : line + 1, :]
                )

    operands = (received, state, extra) + ((passed,) if passed is not None else ())
    outs = [shape(2 * lines, LANES), shape(1, cols)] if first else [shape(lines + 8, LANES)]
    if passed is not None:
        outs.append(shape(*passed.shape))
    return call(body, "own_rows", operands, outs, nbytes=4 * HALF * lines * LANES)


def projected(gathered, own, gathered_first, own_first, lam_old, goal, mass, first, total_cols):
    lines = gathered_first.shape[1] // 2
    blocks = lines // 2

    def body(rows, mine, means, mean, lam_in, target, sums_in, out, lam_out):
        s = scen_index()
        first_row = lax.broadcasted_iota(jnp.int32, (lines, LANES), 0) < blocks

        def folded(values):
            a = jnp.sum(jnp.where(first_row, values, 0.0), 0, keepdims=True)
            b = jnp.sum(jnp.where(first_row, 0.0, values), 0, keepdims=True)
            return jnp.concatenate([a, b], 0)

        def spread(pair):
            return jnp.where(first_row, pair[0:1, :], pair[1:2, :])

        lam = lam_in[...]
        if not first:
            ret = rows[0, lines : lines + 1, 0:K]
            for i in range(1, rows.shape[0]):
                ret = ret + rows[i, lines : lines + 1, 0:K]
            lam = jnp.maximum(lam + STEP_L * (target[...] - ret / total_cols), 0.0)
        lam_out[...] = lam
        slope = STEP_V * spread(jnp.concatenate([picked(lam, s), picked(lam, s + HALF)], 0))
        parts = [
            rows[i, 0:lines, :] + slope * means[i, lines : 2 * lines, :]
            for i in range(rows.shape[0])
        ]
        total = parts[0]
        top = parts[0]
        for part in parts[1:]:
            total = total + part
            top = jnp.maximum(top, part)
        low = jnp.min(top, 0, keepdims=True)
        top_a = jnp.max(jnp.where(first_row, top, low), 0, keepdims=True)
        top_b = jnp.max(jnp.where(first_row, low, top), 0, keepdims=True)
        upper = jnp.max(jnp.concatenate([top_a, top_b], 0), 1, keepdims=True)
        lower = jnp.sum(folded(total), 1, keepdims=True) / total_cols - 1.0

        def excesses(levels):
            found = []
            for level in levels:
                wide = spread(level)
                over = jnp.maximum(parts[0] - wide, 0.0)
                for part in parts[1:]:
                    over = over + jnp.maximum(part - wide, 0.0)
                found.append(folded(over))
            whole = jnp.sum(jnp.concatenate(found, 0), 1, keepdims=True) - total_cols
            return [whole[2 * i : 2 * i + 2, :] for i in range(len(levels))]

        def middles(bounds, depth):
            if depth == 0:
                return None
            low_end, high_end = bounds
            middle = (low_end + high_end) * 0.5
            return (
                middle,
                middles((low_end, middle), depth - 1),
                middles((middle, high_end), depth - 1),
            )

        def listed(tree):
            return [] if tree is None else [tree[0]] + listed(tree[1]) + listed(tree[2])

        def with_values(tree, values):
            if tree is None:
                return None
            return ((tree[0], values.pop(0)), with_values(tree[1], values), with_values(tree[2], values))

        def picked_tree(raise_low, above, below):
            if above is None:
                return None
            node = tuple(jnp.where(raise_low, a, b) for a, b in zip(above[0], below[0]))
            return (
                node,
                picked_tree(raise_low, above[1], below[1]),
                picked_tree(raise_low, above[2], below[2]),
            )

        f_low = None
        f_up = jnp.zeros_like(lower) - total_cols
        for _ in range(BISECT // AHEAD):
            tree = middles((lower, upper), AHEAD)
            levels = listed(tree)
            if f_low is None:
                f_low, *values = excesses([lower] + levels)
            else:
                values = excesses(levels)
            tree = with_values(tree, values)
            while tree is not None:
                (middle, excess), below, above = tree
                raise_low = excess >= 0
                lower = jnp.where(raise_low, middle, lower)
                upper = jnp.where(raise_low, upper, middle)
                f_low = jnp.where(raise_low, excess, f_low)
                f_up = jnp.where(raise_low, f_up, excess)
                tree = picked_tree(raise_low, above, below)
        theta = lower + f_low * (upper - lower) / (f_low - f_up)
        x = mine[0:lines, :] + slope * mean[lines : 2 * lines, :]
        fresh = jnp.maximum(x - spread(theta), 0.0)
        mass = jnp.concatenate([sums_in[...], jnp.zeros((1, LANES - K), F32)], 1)
        for i in range(HALF):
            for half in range(2):
                out[i, 0:blocks, half, :] = fresh[half * blocks : (half + 1) * blocks, :]
                out[i, blocks : blocks + 1, half, :] = mass

    return call(
        body,
        "projected",
        (gathered, own, gathered_first, own_first, lam_old, goal, mass),
        [shape(HALF, blocks + 1, 2, LANES), shape(1, K)],
        nbytes=4 * HALF * HALF * LANES,
    )


def unpacked(received, state, start, mean_row, t_old, last, total_rows):
    cols = state.shape[1]
    blocks = cols // LANES

    def body(got, v, w, m, t, fresh, bars, t_new, t_bar, ret):
        for j in range(blocks):
            at = slice(j * LANES, (j + 1) * LANES)
            fresh[0:HALF, at] = got[:, j, 0, :]
            fresh[HALF:K, at] = got[:, j, 1, :]
        mass = jnp.sum(got[:, blocks, 0, :], 0, keepdims=True)[:, 0:K]
        t_end = t[...] - STEP_T * (1.0 - mass / total_rows / TAIL)
        t_new[...] = t_end
        t_bar[...] = jnp.broadcast_to(in_rows(2.0 * t_end - t[...]), (K, LANES))
        bar = 2.0 * fresh[...] - v[...]
        bars[0:K, :] = (-bar).astype(BF16)
        if not last:
            bars[K : 2 * K, :] = (-w[...]).astype(BF16)
        ret[...] = in_lanes(row_total(lane_folded(bar * m[...])))

    outs = [
        shape(K, cols),
        shape((1 if last else 2) * K, cols, dtype=BF16),
        shape(1, K),
        shape(K, LANES),
        shape(1, K),
    ]
    return call(
        body, "unpacked", (received, state, start, mean_row, t_old), outs, nbytes=20 * K * cols
    )


def mixed(fresh, old, start):
    return (2.0 / 3.0) * (2.0 * fresh - old) + start / 3.0


def averaged(weights, thresholds):
    def body(v2, v1, v0, t2, t1, t0, v_out, t_out):
        v_out[...] = mixed(v2[...], v1[...], v0[...])
        t_out[...] = mixed(t2[...], t1[...], t0[...])

    outs = [shape(*weights[0].shape), shape(1, K)]
    return call(
        body, "averaged", (*weights, *thresholds), outs, nbytes=16 * weights[0].size
    )


def loss_part(bars, returns, sides, quarter, width):
    cols = returns.shape[1]
    count = bars.shape[0] // K

    def body(b, r, *outs):
        for index, side in enumerate(sides):
            base = row_base(side, quarter(), width)
            for i in range(width // TILE):
                at = slice(i * TILE, (i + 1) * TILE)
                block = r[pl.ds(start_of(base + i * TILE), TILE), :]
                term = lax.dot_general(
                    block, b[...], (((1,), (1,)), ((), ())), preferred_element_type=F32
                ).T
                for part in range(count):
                    outs[index * count + part][:, at] = term[part * K : (part + 1) * K, :]

    outs = [shape(K, width)] * (count * len(sides))
    return call(
        body,
        "loss_part",
        (bars, returns),
        outs,
        len(outs) * K * width * cols,
        2 * len(sides) * width * cols,
    )


def plus(a, b):
    def body(x, y, out):
        out[...] = x[...] + y[...]

    return call(body, "plus", (a, b), shape(*a.shape), nbytes=12 * a.size)


def own_and_other(keeps, takes):
    def body(k0, t0, k1, t1, send, keep):
        near = k0[...] + t0[...]
        far = k1[...] + t1[...]
        swap = lax.axis_index("xh") == 0
        send[...] = jnp.where(swap, far, near)
        keep[...] = jnp.where(swap, near, far)

    return call(
        body,
        "own_and_other",
        (keeps[0], takes[0], keeps[1], takes[1]),
        [shape(*keeps[0].shape)] * 2,
        nbytes=24 * keeps[0].size,
    )


def dual_step(loss, duals, t_bar):
    return jnp.clip(duals + STEP_U * (loss - t_bar[:, 0:1]), 0.0, 1.0)


def dual_row(part, other, duals, t_bar, quarter, width):
    def body(p, o, u, t, fresh):
        base = row_base(1, quarter, width)
        fresh[...] = dual_step(p[...] + o[...], u[:, pl.ds(base, width)], t[...])

    return call(body, "dual_row", (part, other, duals, t_bar), shape(K, width), nbytes=16 * K * width)


def gradient_part(terms, returns, before, width):
    cols = returns.shape[1]
    count = len(terms)

    def body(r, *refs):
        fed, rest = refs[:count], refs[count:]
        acc_out, folded_out = rest[-2:]
        total = rest[0][...] if before else None
        folds = rest[1][...] if before else None
        for (_, side, quarter), ref in zip(terms, fed):
            base = row_base(side, quarter, width)
            value = ref[...]
            term = jnp.dot(
                value.astype(BF16), r[pl.ds(base, width), :], preferred_element_type=F32
            )
            total = term if total is None else total + term
            fold = lane_folded(value)
            folds = fold if folds is None else folds + fold
        acc_out[...] = total
        folded_out[...] = folds

    operands = [returns] + [values for values, _, _ in terms] + list(before)
    return call(
        body,
        "gradient_part",
        operands,
        [shape(K, cols), shape(K, LANES)],
        count * K * width * cols,
        2 * count * width * cols,
    )


def gradient_end(taken, side, quarter, returns, before, width):
    cols = returns.shape[1]

    def body(r, got, acc_in, folded_in, out, mass):
        base = row_base(side, quarter, width)
        term = acc_in[...] + jnp.dot(
            got[...].astype(BF16), r[pl.ds(base, width), :], preferred_element_type=F32
        )
        pack(term, out)
        mass[...] = in_lanes(row_total(folded_in[...] + lane_folded(got[...])))

    return call(
        body,
        "gradient_end",
        (returns, taken, *before),
        [packed_shape(cols), shape(1, K)],
        K * width * cols,
        2 * width * cols,
    )


def final_duals(part, other, tails, held, start, t_new, t_old, t_start, t_bar, ret, width):
    devices = 128

    def body(p, o, la, lb, ua, ub, u0, tn, t, ts, tb, er, duals_out, sums):
        mine = lax.axis_index("xh")
        base = row_base(1, mine, width)
        loss = p[...] + o[...]
        old = jnp.where(mine == 0, ua[...], ub[...])
        fresh = dual_step(loss, old, tb[...])
        duals_out[...] = mixed(fresh, old, u0[:, pl.ds(base, width)])
        end = mixed(tn[...], t[...], ts[...])
        tail = (2.0 / 3.0) * loss + (la[...] + lb[...]) / 3.0
        over = jnp.maximum(tail - in_rows(end), 0.0)
        line = jnp.concatenate([in_lanes(row_total(lane_folded(over))), er[...]], 1)
        sums[...] = jnp.broadcast_to(line[None], (devices, 1, LANES))

    operands = (part, other, *tails, *held, start, t_new, t_old, t_start, t_bar, ret)
    return call(
        body,
        "final_duals",
        operands,
        [shape(K, width), shape(devices, 1, LANES)],
        nbytes=24 * K * width,
    )


def joined(pieces, width, ends, total_cols, total_rows):
    devices = ends[0].shape[0]
    copies_of_ret = devices // 4

    def body(
        near, far, own, got, t2, t1, t0, lam_1, lam_0, target, out, tail_out, lam_out, tail, lam, sems
    ):
        mine = lax.axis_index("xh")
        places = ((1, 1 - mine, near), (0, mine, far), (1, mine, own))
        copies = []
        for i, (side, quarter, ref) in enumerate(places):
            to = out.at[:, pl.ds(row_base(side, quarter, width), width)]
            copies.append(pltpu.make_async_copy(ref, to, sems.at[i]))
        for copy in copies:
            copy.start()
        total = jnp.sum(got[...], 0)
        end = mixed(t2[...], t1[...], t0[...])
        tail[...] = end + total[:, 0:K] / (TAIL * total_rows)
        ret = total[:, K : 2 * K] / copies_of_ret
        fresh = jnp.maximum(lam_1[...] + STEP_L * (target[...] - ret / total_cols), 0.0)
        lam[...] = mixed(fresh, lam_1[...], lam_0[...])
        for ref, to in ((tail, tail_out), (lam, lam_out)):
            copies.append(pltpu.make_async_copy(ref, to, sems.at[len(copies)]))
            copies[-1].start()
        for copy in copies:
            copy.wait()

    return call(
        body,
        "joined",
        (*pieces, *ends),
        [pltpu.HBM((K, 4 * width), F32), pltpu.HBM((1, K), F32), pltpu.HBM((1, K), F32)],
        nbytes=24 * K * width,
        scratch=(
            pltpu.VMEM((1, K), F32),
            pltpu.VMEM((1, K), F32),
            pltpu.SemaphoreType.DMA((5,)),
        ),
        out_specs=[ANY] * 3,
    )


def completed(duals_out, last, width):
    def body(before, piece, out, sem):
        to = out.at[:, pl.ds(row_base(0, 1 - lax.axis_index("xh"), width), width)]
        copy = pltpu.make_async_copy(piece, to, sem)
        copy.start()
        copy.wait()

    return call(
        body,
        "completed",
        (duals_out, last),
        pltpu.HBM(duals_out.shape, F32),
        nbytes=8 * K * width,
        scratch=(pltpu.SemaphoreType.DMA,),
        in_specs=[ANY, VMEM],
        out_specs=ANY,
        aliases={0: 0},
    )


def pinned(a):
    return pltpu.with_memory_space_constraint(a, pltpu.VMEM)


def across(values, axis):
    return lax.ppermute(values, axis, [(0, 1), (1, 0)])


def plus_gathered(a, both):
    def body(x, y, out):
        core = lax.axis_index("core")
        out[...] = x[...] + y[1 - core]

    return call(body, "plus", (a, both), shape(*a.shape), nbytes=12 * a.size)


def exchanged(payload, others):
    payload, others = lax.optimization_barrier((payload, others))
    received = lax.all_to_all(payload, SCEN, 0, 0)
    return lax.optimization_barrier((received, others))


def local(returns, mean_return, targets, weights, threshold, duals, multiplier):
    scen_rows, cols = returns.shape
    total_cols = cols * 4
    total_rows = scen_rows * 32
    width = scen_rows // 4
    t0 = threshold.reshape(1, K)
    lam0 = multiplier.reshape(1, K)
    goal = targets.reshape(1, K)

    payload, mass, returns, duals = first_gradient(duals, returns)
    returns = pinned(returns)
    held = (returns, duals, weights, mean_return, t0, lam0, goal, mass)
    received, held = exchanged(payload, held)
    returns, duals, weights, mean_return, t0, lam0, goal, mass = held
    own_first, mean_row = own_rows(
        received, weights, mean_return, None, True, total_cols, total_rows
    )
    gathered_first = lax.all_gather(own_first, ASSET)
    payload, lam0 = projected(
        gathered_first, own_first, gathered_first, own_first, lam0, goal, mass, True, total_cols
    )
    held = (returns, duals, weights, mean_row, t0, lam0, goal, gathered_first, own_first)
    received, held = exchanged(payload, held)
    returns, duals, weights, mean_row, t0, lam0, goal, gathered_first, own_first = held
    returns = pinned(returns)
    v1, bars, t1, bar1, ret1 = unpacked(
        received, weights, weights, mean_row, t0, False, total_rows
    )

    send, send_tail_a = loss_part(bars, returns, (0,), lambda: 0, width)
    take = across(send, "core")
    keep, keep_tail_a = loss_part(bars, returns, (1,), lambda: 0, width)
    part_a = plus(keep, take)
    take_tail_a = across(send_tail_a, "core")
    part_a, bars = lax.optimization_barrier((part_a, bars))
    send, send_tail_b, keep, keep_tail_b = loss_part(bars, returns, (0, 1), lambda: 1, width)
    part_b = plus_gathered(keep, lax.all_gather(send, "core"))
    take_tail_b = across(send_tail_b, "core")
    others = (across(part_a, "xh"), across(part_b, "xh"))
    send_tail, tail_a = own_and_other((keep_tail_a, keep_tail_b), (take_tail_a, take_tail_b))

    ua = dual_row(part_a, others[0], duals, bar1, 0, width)
    taken_a = across(ua, "core")
    ub = dual_row(part_b, others[1], duals, bar1, 1, width)
    ub, send_tail = lax.optimization_barrier((ub, send_tail))
    taken_b = across(ub, "core")
    sums = gradient_part([(ua, 1, 0), (ub, 1, 1)], returns, (), width)
    sums = gradient_part([(taken_a, 0, 0)], returns, sums, width)
    payload, mass = gradient_end(taken_b, 0, 1, returns, sums, width)

    held = (returns, duals, weights, mean_row, v1, t0, t1, lam0, goal, gathered_first, own_first)
    held = held + (ret1, ua, ub, tail_a, send_tail, mass)
    received, held = exchanged(payload, held)
    returns, duals, weights, mean_row, v1, t0, t1, lam0, goal, gathered_first, own_first = held[:11]
    ret1, ua, ub, tail_a, send_tail, mass = held[11:]
    own, send_tail = own_rows(received, v1, ret1, send_tail, False, total_cols, total_rows)
    tail_b = across(send_tail, "xh")
    gathered = lax.all_gather(own, ASSET)
    payload, lam1 = projected(
        gathered, own, gathered_first, own_first, lam0, goal, mass, False, total_cols
    )
    held = (returns, duals, weights, mean_row, v1, t0, t1, lam0, lam1, goal, ua, ub, tail_a, tail_b)
    received, held = exchanged(payload, held)
    returns, duals, weights, mean_row, v1, t0, t1, lam0, lam1, goal, ua, ub, tail_a, tail_b = held
    returns = pinned(returns)
    v2, bars, t2, bar2, ret2 = unpacked(received, v1, weights, mean_row, t1, True, total_rows)

    def far_quarter():
        return 1 - lax.axis_index("xh")

    def own_quarter():
        return lax.axis_index("xh")

    (send,) = loss_part(bars, returns, (0,), far_quarter, width)
    take = across(send, "core")
    (keep,) = loss_part(bars, returns, (1,), far_quarter, width)
    part_a = plus(keep, take)
    part_a, bars, v2 = lax.optimization_barrier((part_a, bars, v2))
    send, keep = loss_part(bars, returns, (0, 1), own_quarter, width)
    part_b = plus_gathered(keep, lax.all_gather(send, "core"))
    parts = (part_a, part_b)
    other = across(parts[0], "xh")
    weights_out, threshold_out = averaged((v2, v1, weights), (t2, t1, t0))
    part, weights_out = lax.optimization_barrier((parts[1], weights_out))

    quarter, sums = final_duals(
        part, other, (tail_a, tail_b), (ua, ub), duals, t2, t1, t0, bar2, ret2, width
    )
    near = across(quarter, "xh")
    far = across(quarter, "core")
    sums = lax.all_to_all(sums, ALL, 0, 0)
    near, far, sums = lax.optimization_barrier((near, far, sums))
    far_near = across(near, "core")
    ends = (sums, t2, t1, t0, lam1, lam0, goal)
    duals_out, tail_risk, lam_out = joined(
        (near, far, quarter), width, ends, total_cols, total_rows
    )
    duals_out = completed(duals_out, far_near, width)
    return (weights_out, threshold_out.reshape(K), duals_out, lam_out.reshape(K), tail_risk.reshape(K))


def solution(mesh):
    split = Mesh(mesh.devices.reshape(4, 4, 2, 2, 2), ALL)
    in_specs = (P(SCEN, ASSET), P(ASSET), P(), P(None, ASSET), P(), P(None, SCEN), P())
    out_specs = (P(None, ASSET), P(), P(None, SCEN), P(), P())
    return jax.shard_map(local, mesh=split, in_specs=in_specs, out_specs=out_specs, check_vma=False)
```

```python
import math

import jax
import jax.numpy as jnp
from jax import lax
from jax.experimental import pallas as pl
from jax.experimental.pallas import tpu as pltpu
from jax.sharding import Mesh
from jax.sharding import PartitionSpec as P

BISECT = 6
AHEAD = 3
TAIL = 0.2
STEP_V = 1.0
STEP_T = 0.5
STEP_U = 0.5
STEP_L = 2.0

SCEN = ("z", "y", "xl")
ASSET = ("xh", "core")
ALL = SCEN + ASSET

K = 64
HALF = 32
LANES = 128
TILE = 768
FIRST_TILE = 384

F32 = jnp.float32
BF16 = jnp.bfloat16

VMEM = pl.BlockSpec(memory_space=pltpu.VMEM)
SMEM = pl.BlockSpec(memory_space=pltpu.SMEM)
ANY = pl.BlockSpec(memory_space=pl.ANY)


def params():
    return pltpu.CompilerParams(vmem_limit_bytes=12 << 20)


def shape(*dims, dtype=F32):
    return jax.ShapeDtypeStruct(dims, dtype)


def cost(macs, nbytes):
    return pl.CostEstimate(flops=2 * macs // 100, bytes_accessed=nbytes // 100, transcendentals=0)


def start_of(offset):
    return pl.multiple_of(offset, LANES)


def lane_folded(values):
    total = values[:, 0:LANES]
    for j in range(1, values.shape[1] // LANES):
        total = total + values[:, j * LANES : (j + 1) * LANES]
    return total


def row_total(folded):
    return jnp.broadcast_to(jnp.sum(folded, 1, keepdims=True), folded.shape)


def diagonal(rows, first=0):
    return lax.broadcasted_iota(jnp.int32, (rows, LANES), 1) == first + lax.broadcasted_iota(
        jnp.int32, (rows, LANES), 0
    )


def in_lanes(column):
    return jnp.sum(jnp.where(diagonal(K), column, 0.0), 0, keepdims=True)[:, 0:K]


def in_rows(line):
    square = diagonal(K)[:, 0:K]
    return jnp.sum(jnp.where(square, jnp.broadcast_to(line, (K, K)), 0.0), 1, keepdims=True)


def picked(line, row):
    at = lax.broadcasted_iota(jnp.int32, line.shape, 1) == row
    return jnp.sum(jnp.where(at, line, 0.0), 1, keepdims=True)


def row_base(core_side, quarter, width):
    core = lax.axis_index("core")
    half = core if core_side else 1 - core
    return start_of((half * 2 + quarter) * width)


def scen_index():
    return (lax.axis_index("z") * 4 + lax.axis_index("y")) * 2 + lax.axis_index("xl")


def call(
    body, name, operands, outs, macs=0, nbytes=0, scratch=(), in_specs=None, out_specs=None, aliases=None
):
    single = not isinstance(outs, list)
    return pl.pallas_call(
        body,
        in_specs=in_specs or [VMEM] * len(operands),
        out_specs=out_specs or (VMEM if single else [VMEM] * len(outs)),
        input_output_aliases=aliases or {},
        out_shape=outs,
        scratch_shapes=list(scratch),
        compiler_params=params(),
        cost_estimate=cost(macs, nbytes),
        name=name,
    )(*operands)


def pack(acc, out):
    blocks = acc.shape[1] // LANES
    for j in range(blocks):
        out[:, j, :] = acc[0:HALF, j * LANES : (j + 1) * LANES]
        out[:, blocks + j, :] = acc[HALF:K, j * LANES : (j + 1) * LANES]


def packed_shape(cols):
    return shape(HALF, 2 * cols // LANES, LANES)


def first_gradient(duals, returns):
    rows, cols = returns.shape
    steps = rows // FIRST_TILE

    def body(u, r, out, mass, held, kept, acc, sems, dual_sems):
        copies = []
        for i in range(steps):
            at = pl.ds(i * FIRST_TILE, FIRST_TILE)
            mine = pltpu.make_async_copy(u.at[:, at], kept.at[:, at], dual_sems.at[i])
            block = pltpu.make_async_copy(r.at[at], held.at[at], sems.at[i])
            mine.start()
            block.start()
            copies.append((mine, block))
        folded = jnp.zeros((K, LANES), F32)
        for i in range(steps):
            copies[i][0].wait()
            part = kept[:, i * FIRST_TILE : (i + 1) * FIRST_TILE]
            folded = folded + lane_folded(part)
            copies[i][1].wait()
            term = jnp.dot(
                part.astype(BF16), held[pl.ds(i * FIRST_TILE, FIRST_TILE), :], preferred_element_type=F32
            )
            acc[...] = term if i == 0 else acc[...] + term
        pack(acc[...], out)
        mass[...] = in_lanes(row_total(folded))

    operands = [pltpu.with_memory_space_constraint(a, pltpu.HBM) for a in (duals, returns)]
    outs = [
        packed_shape(cols),
        shape(1, K),
        pltpu.VMEM((rows, cols), BF16),
        pltpu.VMEM((K, rows), F32),
    ]
    scratch = (
        pltpu.VMEM((K, cols), F32),
        pltpu.SemaphoreType.DMA((steps,)),
        pltpu.SemaphoreType.DMA((steps,)),
    )
    return call(
        body, "first_gradient", operands, outs, K * rows * cols, 2 * rows * cols, scratch, [ANY, ANY]
    )


def own_rows(received, state, extra, passed, first, total_cols, total_rows):
    scale = math.sqrt(total_cols / total_rows)
    cols = state.shape[1]
    blocks = cols // LANES
    lines = 2 * blocks

    def body(got, v, more, *refs):
        s = scen_index()
        grad = jnp.sum(got[...], 0)
        if first:
            out, line_out = refs
            for j in range(blocks):
                piece = more[pl.ds(j * LANES, LANES)].reshape(1, LANES)
                line_out[:, j * LANES : (j + 1) * LANES] = piece
                out[lines + j : lines + j + 1, :] = piece
                out[lines + blocks + j : lines + blocks + j + 1, :] = piece
        else:
            through, out, through_out = refs
            through_out[...] = through[...]
            out[lines:, :] = jnp.zeros((out.shape[0] - lines, LANES), F32)
            out[lines : lines + 1, 0:K] = more[...]
        for half in range(2):
            values = v[half * HALF : (half + 1) * HALF, :]
            at = lax.broadcasted_iota(jnp.int32, values.shape, 0) == s
            old = jnp.sum(jnp.where(at, values, 0.0), 0, keepdims=True)
            for j in range(blocks):
                line = half * blocks + j
                out[line : line + 1, :] = (
                    old[:, j * LANES : (j + 1) * LANES] + STEP_V * scale * grad[line : line + 1, :]
                )

    operands = (received, state, extra) + ((passed,) if passed is not None else ())
    outs = [shape(2 * lines, LANES), shape(1, cols)] if first else [shape(lines + 8, LANES)]
    if passed is not None:
        outs.append(shape(*passed.shape))
    return call(body, "own_rows", operands, outs, nbytes=4 * HALF * lines * LANES)


def projected(gathered, own, gathered_first, own_first, lam_old, goal, mass, first, total_cols):
    lines = gathered_first.shape[1] // 2
    blocks = lines // 2

    def body(rows, mine, means, mean, lam_in, target, sums_in, out, lam_out):
        s = scen_index()
        first_row = lax.broadcasted_iota(jnp.int32, (lines, LANES), 0) < blocks

        def folded(values):
            a = jnp.sum(jnp.where(first_row, values, 0.0), 0, keepdims=True)
            b = jnp.sum(jnp.where(first_row, 0.0, values), 0, keepdims=True)
            return jnp.concatenate([a, b], 0)

        def spread(pair):
            return jnp.where(first_row, pair[0:1, :], pair[1:2, :])

        lam = lam_in[...]
        if not first:
            ret = rows[0, lines : lines + 1, 0:K]
            for i in range(1, rows.shape[0]):
                ret = ret + rows[i, lines : lines + 1, 0:K]
            lam = jnp.maximum(lam + STEP_L * (target[...] - ret / total_cols), 0.0)
        lam_out[...] = lam
        slope = STEP_V * spread(jnp.concatenate([picked(lam, s), picked(lam, s + HALF)], 0))
        parts = [
            rows[i, 0:lines, :] + slope * means[i, lines : 2 * lines, :]
            for i in range(rows.shape[0])
        ]
        total = parts[0]
        top = parts[0]
        for part in parts[1:]:
            total = total + part
            top = jnp.maximum(top, part)
        low = jnp.min(top, 0, keepdims=True)
        top_a = jnp.max(jnp.where(first_row, top, low), 0, keepdims=True)
        top_b = jnp.max(jnp.where(first_row, low, top), 0, keepdims=True)
        upper = jnp.max(jnp.concatenate([top_a, top_b], 0), 1, keepdims=True)
        lower = jnp.sum(folded(total), 1, keepdims=True) / total_cols - 1.0

        def excesses(levels):
            found = []
            for level in levels:
                wide = spread(level)
                over = jnp.maximum(parts[0] - wide, 0.0)
                for part in parts[1:]:
                    over = over + jnp.maximum(part - wide, 0.0)
                found.append(folded(over))
            whole = jnp.sum(jnp.concatenate(found, 0), 1, keepdims=True) - total_cols
            return [whole[2 * i : 2 * i + 2, :] for i in range(len(levels))]

        def middles(bounds, depth):
            if depth == 0:
                return None
            low_end, high_end = bounds
            middle = (low_end + high_end) * 0.5
            return (
                middle,
                middles((low_end, middle), depth - 1),
                middles((middle, high_end), depth - 1),
            )

        def listed(tree):
            return [] if tree is None else [tree[0]] + listed(tree[1]) + listed(tree[2])

        def with_values(tree, values):
            if tree is None:
                return None
            return ((tree[0], values.pop(0)), with_values(tree[1], values), with_values(tree[2], values))

        def picked_tree(raise_low, above, below):
            if above is None:
                return None
            node = tuple(jnp.where(raise_low, a, b) for a, b in zip(above[0], below[0]))
            return (
                node,
                picked_tree(raise_low, above[1], below[1]),
                picked_tree(raise_low, above[2], below[2]),
            )

        f_low = None
        f_up = jnp.zeros_like(lower) - total_cols
        for _ in range(BISECT // AHEAD):
            tree = middles((lower, upper), AHEAD)
            levels = listed(tree)
            if f_low is None:
                f_low, *values = excesses([lower] + levels)
            else:
                values = excesses(levels)
            tree = with_values(tree, values)
            while tree is not None:
                (middle, excess), below, above = tree
                raise_low = excess >= 0
                lower = jnp.where(raise_low, middle, lower)
                upper = jnp.where(raise_low, upper, middle)
                f_low = jnp.where(raise_low, excess, f_low)
                f_up = jnp.where(raise_low, f_up, excess)
                tree = picked_tree(raise_low, above, below)
        theta = lower + f_low * (upper - lower) / (f_low - f_up)
        x = mine[0:lines, :] + slope * mean[lines : 2 * lines, :]
        fresh = jnp.maximum(x - spread(theta), 0.0)
        mass = jnp.concatenate([sums_in[...], jnp.zeros((1, LANES - K), F32)], 1)
        for i in range(HALF):
            for half in range(2):
                out[i, 0:blocks, half, :] = fresh[half * blocks : (half + 1) * blocks, :]
                out[i, blocks : blocks + 1, half, :] = mass

    return call(
        body,
        "projected",
        (gathered, own, gathered_first, own_first, lam_old, goal, mass),
        [shape(HALF, blocks + 1, 2, LANES), shape(1, K)],
        nbytes=4 * HALF * HALF * LANES,
    )


def unpacked(received, state, start, mean_row, t_old, last, total_rows):
    cols = state.shape[1]
    blocks = cols // LANES

    def body(got, v, w, m, t, fresh, bars, t_new, t_bar, ret):
        for j in range(blocks):
            at = slice(j * LANES, (j + 1) * LANES)
            fresh[0:HALF, at] = got[:, j, 0, :]
            fresh[HALF:K, at] = got[:, j, 1, :]
        mass = jnp.sum(got[:, blocks, 0, :], 0, keepdims=True)[:, 0:K]
        t_end = t[...] - STEP_T * (1.0 - mass / total_rows / TAIL)
        t_new[...] = t_end
        t_bar[...] = jnp.broadcast_to(in_rows(2.0 * t_end - t[...]), (K, LANES))
        bar = 2.0 * fresh[...] - v[...]
        bars[0:K, :] = (-bar).astype(BF16)
        if not last:
            bars[K : 2 * K, :] = (-w[...]).astype(BF16)
        ret[...] = in_lanes(row_total(lane_folded(bar * m[...])))

    outs = [
        shape(K, cols),
        shape((1 if last else 2) * K, cols, dtype=BF16),
        shape(1, K),
        shape(K, LANES),
        shape(1, K),
    ]
    return call(
        body, "unpacked", (received, state, start, mean_row, t_old), outs, nbytes=20 * K * cols
    )


def mixed(fresh, old, start):
    return (2.0 / 3.0) * (2.0 * fresh - old) + start / 3.0


def averaged(weights, thresholds):
    def body(v2, v1, v0, t2, t1, t0, v_out, t_out):
        v_out[...] = mixed(v2[...], v1[...], v0[...])
        t_out[...] = mixed(t2[...], t1[...], t0[...])

    outs = [shape(*weights[0].shape), shape(1, K)]
    return call(
        body, "averaged", (*weights, *thresholds), outs, nbytes=16 * weights[0].size
    )


def loss_part(bars, returns, sides, quarter, width):
    cols = returns.shape[1]
    count = bars.shape[0] // K

    def body(b, r, *outs):
        for index, side in enumerate(sides):
            base = row_base(side, quarter(), width)
            for i in range(width // TILE):
                at = slice(i * TILE, (i + 1) * TILE)
                block = r[pl.ds(start_of(base + i * TILE), TILE), :]
                term = lax.dot_general(
                    block, b[...], (((1,), (1,)), ((), ())), preferred_element_type=F32
                ).T
                for part in range(count):
                    outs[index * count + part][:, at] = term[part * K : (part + 1) * K, :]

    outs = [shape(K, width)] * (count * len(sides))
    return call(
        body,
        "loss_part",
        (bars, returns),
        outs,
        len(outs) * K * width * cols,
        2 * len(sides) * width * cols,
    )


def plus(a, b):
    def body(x, y, out):
        out[...] = x[...] + y[...]

    return call(body, "plus", (a, b), shape(*a.shape), nbytes=12 * a.size)


def own_and_other(keeps, takes):
    def body(k0, t0, k1, t1, send, keep):
        near = k0[...] + t0[...]
        far = k1[...] + t1[...]
        swap = lax.axis_index("xh") == 0
        send[...] = jnp.where(swap, far, near)
        keep[...] = jnp.where(swap, near, far)

    return call(
        body,
        "own_and_other",
        (keeps[0], takes[0], keeps[1], takes[1]),
        [shape(*keeps[0].shape)] * 2,
        nbytes=24 * keeps[0].size,
    )


def dual_step(loss, duals, t_bar):
    return jnp.clip(duals + STEP_U * (loss - t_bar[:, 0:1]), 0.0, 1.0)


def dual_row(part, other, duals, t_bar, quarter, width):
    def body(p, o, u, t, fresh):
        base = row_base(1, quarter, width)
        fresh[...] = dual_step(p[...] + o[...], u[:, pl.ds(base, width)], t[...])

    return call(body, "dual_row", (part, other, duals, t_bar), shape(K, width), nbytes=16 * K * width)


def gradient_part(terms, returns, before, width):
    cols = returns.shape[1]
    count = len(terms)

    def body(r, *refs):
        fed, rest = refs[:count], refs[count:]
        acc_out, folded_out = rest[-2:]
        total = rest[0][...] if before else None
        folds = rest[1][...] if before else None
        for (_, side, quarter), ref in zip(terms, fed):
            base = row_base(side, quarter, width)
            value = ref[...]
            term = jnp.dot(
                value.astype(BF16), r[pl.ds(base, width), :], preferred_element_type=F32
            )
            total = term if total is None else total + term
            fold = lane_folded(value)
            folds = fold if folds is None else folds + fold
        acc_out[...] = total
        folded_out[...] = folds

    operands = [returns] + [values for values, _, _ in terms] + list(before)
    return call(
        body,
        "gradient_part",
        operands,
        [shape(K, cols), shape(K, LANES)],
        count * K * width * cols,
        2 * count * width * cols,
    )


def gradient_end(taken, side, quarter, returns, before, width):
    cols = returns.shape[1]

    def body(r, got, acc_in, folded_in, out, mass):
        base = row_base(side, quarter, width)
        term = acc_in[...] + jnp.dot(
            got[...].astype(BF16), r[pl.ds(base, width), :], preferred_element_type=F32
        )
        pack(term, out)
        mass[...] = in_lanes(row_total(folded_in[...] + lane_folded(got[...])))

    return call(
        body,
        "gradient_end",
        (returns, taken, *before),
        [packed_shape(cols), shape(1, K)],
        K * width * cols,
        2 * width * cols,
    )


def final_duals(part, other, tails, held, start, t_new, t_old, t_start, t_bar, ret, width):
    devices = 128

    def body(p, o, la, lb, ua, ub, u0, tn, t, ts, tb, er, duals_out, sums):
        mine = lax.axis_index("xh")
        base = row_base(1, mine, width)
        loss = p[...] + o[...]
        old = jnp.where(mine == 0, ua[...], ub[...])
        fresh = dual_step(loss, old, tb[...])
        duals_out[...] = mixed(fresh, old, u0[:, pl.ds(base, width)])
        end = mixed(tn[...], t[...], ts[...])
        tail = (2.0 / 3.0) * loss + (la[...] + lb[...]) / 3.0
        over = jnp.maximum(tail - in_rows(end), 0.0)
        line = jnp.concatenate([in_lanes(row_total(lane_folded(over))), er[...]], 1)
        sums[...] = jnp.broadcast_to(line[None], (devices, 1, LANES))

    operands = (part, other, *tails, *held, start, t_new, t_old, t_start, t_bar, ret)
    return call(
        body,
        "final_duals",
        operands,
        [shape(K, width), shape(devices, 1, LANES)],
        nbytes=24 * K * width,
    )


def joined(pieces, width, ends, total_cols, total_rows):
    devices = ends[0].shape[0]
    copies_of_ret = devices // 4

    def body(
        near, far, own, got, t2, t1, t0, lam_1, lam_0, target, out, tail_out, lam_out, tail, lam, sems
    ):
        mine = lax.axis_index("xh")
        places = ((1, 1 - mine, near), (0, mine, far), (1, mine, own))
        copies = []
        for i, (side, quarter, ref) in enumerate(places):
            to = out.at[:, pl.ds(row_base(side, quarter, width), width)]
            copies.append(pltpu.make_async_copy(ref, to, sems.at[i]))
        for copy in copies:
            copy.start()
        total = jnp.sum(got[...], 0)
        end = mixed(t2[...], t1[...], t0[...])
        tail[...] = end + total[:, 0:K] / (TAIL * total_rows)
        ret = total[:, K : 2 * K] / copies_of_ret
        fresh = jnp.maximum(lam_1[...] + STEP_L * (target[...] - ret / total_cols), 0.0)
        lam[...] = mixed(fresh, lam_1[...], lam_0[...])
        for ref, to in ((tail, tail_out), (lam, lam_out)):
            copies.append(pltpu.make_async_copy(ref, to, sems.at[len(copies)]))
            copies[-1].start()
        for copy in copies:
            copy.wait()

    return call(
        body,
        "joined",
        (*pieces, *ends),
        [pltpu.HBM((K, 4 * width), F32), pltpu.HBM((1, K), F32), pltpu.HBM((1, K), F32)],
        nbytes=24 * K * width,
        scratch=(
            pltpu.VMEM((1, K), F32),
            pltpu.VMEM((1, K), F32),
            pltpu.SemaphoreType.DMA((5,)),
        ),
        out_specs=[ANY] * 3,
    )


def completed(duals_out, last, width):
    def body(before, piece, out, sem):
        to = out.at[:, pl.ds(row_base(0, 1 - lax.axis_index("xh"), width), width)]
        copy = pltpu.make_async_copy(piece, to, sem)
        copy.start()
        copy.wait()

    return call(
        body,
        "completed",
        (duals_out, last),
        pltpu.HBM(duals_out.shape, F32),
        nbytes=8 * K * width,
        scratch=(pltpu.SemaphoreType.DMA,),
        in_specs=[ANY, VMEM],
        out_specs=ANY,
        aliases={0: 0},
    )


def pinned(a):
    return pltpu.with_memory_space_constraint(a, pltpu.VMEM)


def across(values, axis):
    return lax.ppermute(values, axis, [(0, 1), (1, 0)])


def plus_gathered(a, both):
    def body(x, y, out):
        core = lax.axis_index("core")
        out[...] = x[...] + y[1 - core]

    return call(body, "plus", (a, both), shape(*a.shape), nbytes=12 * a.size)


def exchanged(payload, others):
    payload, others = lax.optimization_barrier((payload, others))
    received = lax.all_to_all(payload, SCEN, 0, 0)
    return lax.optimization_barrier((received, others))


def local(returns, mean_return, targets, weights, threshold, duals, multiplier):
    scen_rows, cols = returns.shape
    total_cols = cols * 4
    total_rows = scen_rows * 32
    width = scen_rows // 4
    t0 = threshold.reshape(1, K)
    lam0 = multiplier.reshape(1, K)
    goal = targets.reshape(1, K)

    payload, mass, returns, duals = first_gradient(duals, returns)
    returns = pinned(returns)
    held = (returns, duals, weights, mean_return, t0, lam0, goal, mass)
    received, held = exchanged(payload, held)
    returns, duals, weights, mean_return, t0, lam0, goal, mass = held
    own_first, mean_row = own_rows(
        received, weights, mean_return, None, True, total_cols, total_rows
    )
    gathered_first = lax.all_gather(own_first, ASSET)
    payload, lam0 = projected(
        gathered_first, own_first, gathered_first, own_first, lam0, goal, mass, True, total_cols
    )
    held = (returns, duals, weights, mean_row, t0, lam0, goal, gathered_first, own_first)
    received, held = exchanged(payload, held)
    returns, duals, weights, mean_row, t0, lam0, goal, gathered_first, own_first = held
    returns = pinned(returns)
    v1, bars, t1, bar1, ret1 = unpacked(
        received, weights, weights, mean_row, t0, False, total_rows
    )

    send, send_tail_a = loss_part(bars, returns, (0,), lambda: 0, width)
    take = across(send, "core")
    keep, keep_tail_a = loss_part(bars, returns, (1,), lambda: 0, width)
    part_a = plus(keep, take)
    take_tail_a = across(send_tail_a, "core")
    part_a, bars = lax.optimization_barrier((part_a, bars))
    send, send_tail_b, keep, keep_tail_b = loss_part(bars, returns, (0, 1), lambda: 1, width)
    part_b = plus_gathered(keep, lax.all_gather(send, "core"))
    take_tail_b = across(send_tail_b, "core")
    others = (across(part_a, "xh"), across(part_b, "xh"))
    send_tail, tail_a = own_and_other((keep_tail_a, keep_tail_b), (take_tail_a, take_tail_b))

    ua = dual_row(part_a, others[0], duals, bar1, 0, width)
    taken_a = across(ua, "core")
    ub = dual_row(part_b, others[1], duals, bar1, 1, width)
    ub, send_tail = lax.optimization_barrier((ub, send_tail))
    taken_b = across(ub, "core")
    sums = gradient_part([(ua, 1, 0), (ub, 1, 1)], returns, (), width)
    sums = gradient_part([(taken_a, 0, 0)], returns, sums, width)
    payload, mass = gradient_end(taken_b, 0, 1, returns, sums, width)

    held = (returns, duals, weights, mean_row, v1, t0, t1, lam0, goal, gathered_first, own_first)
    held = held + (ret1, ua, ub, tail_a, send_tail, mass)
    received, held = exchanged(payload, held)
    returns, duals, weights, mean_row, v1, t0, t1, lam0, goal, gathered_first, own_first = held[:11]
    ret1, ua, ub, tail_a, send_tail, mass = held[11:]
    own, send_tail = own_rows(received, v1, ret1, send_tail, False, total_cols, total_rows)
    tail_b = across(send_tail, "xh")
    gathered = lax.all_gather(own, ASSET)
    payload, lam1 = projected(
        gathered, own, gathered_first, own_first, lam0, goal, mass, False, total_cols
    )
    held = (returns, duals, weights, mean_row, v1, t0, t1, lam0, lam1, goal, ua, ub, tail_a, tail_b)
    received, held = exchanged(payload, held)
    returns, duals, weights, mean_row, v1, t0, t1, lam0, lam1, goal, ua, ub, tail_a, tail_b = held
    returns = pinned(returns)
    v2, bars, t2, bar2, ret2 = unpacked(received, v1, weights, mean_row, t1, True, total_rows)

    def far_quarter():
        return 1 - lax.axis_index("xh")

    def own_quarter():
        return lax.axis_index("xh")

    (send,) = loss_part(bars, returns, (0,), far_quarter, width)
    take = across(send, "core")
    (keep,) = loss_part(bars, returns, (1,), far_quarter, width)
    part_a = plus(keep, take)
    part_a, bars, v2 = lax.optimization_barrier((part_a, bars, v2))
    send, keep = loss_part(bars, returns, (0, 1), own_quarter, width)
    part_b = plus_gathered(keep, lax.all_gather(send, "core"))
    parts = (part_a, part_b)
    other = across(parts[0], "xh")
    weights_out, threshold_out = averaged((v2, v1, weights), (t2, t1, t0))
    part, weights_out = lax.optimization_barrier((parts[1], weights_out))

    quarter, sums = final_duals(
        part, other, (tail_a, tail_b), (ua, ub), duals, t2, t1, t0, bar2, ret2, width
    )
    near = across(quarter, "xh")
    far = across(quarter, "core")
    sums = lax.all_to_all(sums, ALL, 0, 0)
    near, far, sums = lax.optimization_barrier((near, far, sums))
    far_near = across(near, "core")
    ends = (sums, t2, t1, t0, lam1, lam0, goal)
    duals_out, tail_risk, lam_out = joined(
        (near, far, quarter), width, ends, total_cols, total_rows
    )
    duals_out = completed(duals_out, far_near, width)
    return (weights_out, threshold_out.reshape(K), duals_out, lam_out.reshape(K), tail_risk.reshape(K))


def solution(mesh):
    split = Mesh(mesh.devices.reshape(4, 4, 2, 2, 2), ALL)
    in_specs = (P(SCEN, ASSET), P(ASSET), P(), P(None, ASSET), P(), P(None, SCEN), P())
    out_specs = (P(None, ASSET), P(), P(None, SCEN), P(), P())
    return jax.shard_map(local, mesh=split, in_specs=in_specs, out_specs=out_specs, check_vma=False)
```

```python
import math

import jax
import jax.numpy as jnp
from jax import lax
from jax.experimental import pallas as pl
from jax.experimental.pallas import tpu as pltpu
from jax.sharding import Mesh
from jax.sharding import PartitionSpec as P

BISECT = 6
AHEAD = 3
TAIL = 0.2
STEP_V = 1.0
STEP_T = 0.5
STEP_U = 0.5
STEP_L = 2.0

SCEN = ("z", "y", "xl")
ASSET = ("xh", "core")
ALL = SCEN + ASSET

K = 64
HALF = 32
LANES = 128
TILE = 768

F32 = jnp.float32
BF16 = jnp.bfloat16

VMEM = pl.BlockSpec(memory_space=pltpu.VMEM)
SMEM = pl.BlockSpec(memory_space=pltpu.SMEM)
ANY = pl.BlockSpec(memory_space=pl.ANY)


def params():
    return pltpu.CompilerParams(vmem_limit_bytes=12 << 20)


def shape(*dims, dtype=F32):
    return jax.ShapeDtypeStruct(dims, dtype)


def cost(macs, nbytes):
    return pl.CostEstimate(flops=2 * macs // 100, bytes_accessed=nbytes // 100, transcendentals=0)


def start_of(offset):
    return pl.multiple_of(offset, LANES)


def lane_folded(values):
    total = values[:, 0:LANES]
    for j in range(1, values.shape[1] // LANES):
        total = total + values[:, j * LANES : (j + 1) * LANES]
    return total


def row_total(folded):
    return jnp.broadcast_to(jnp.sum(folded, 1, keepdims=True), folded.shape)


def diagonal(rows, first=0):
    return lax.broadcasted_iota(jnp.int32, (rows, LANES), 1) == first + lax.broadcasted_iota(
        jnp.int32, (rows, LANES), 0
    )


def in_lanes(column):
    return jnp.sum(jnp.where(diagonal(K), column, 0.0), 0, keepdims=True)[:, 0:K]


def in_rows(line):
    square = diagonal(K)[:, 0:K]
    return jnp.sum(jnp.where(square, jnp.broadcast_to(line, (K, K)), 0.0), 1, keepdims=True)


def picked(line, row):
    at = lax.broadcasted_iota(jnp.int32, line.shape, 1) == row
    return jnp.sum(jnp.where(at, line, 0.0), 1, keepdims=True)


def row_base(core_side, quarter, width):
    core = lax.axis_index("core")
    half = core if core_side else 1 - core
    return start_of((half * 2 + quarter) * width)


def scen_index():
    return (lax.axis_index("z") * 4 + lax.axis_index("y")) * 2 + lax.axis_index("xl")


def call(
    body, name, operands, outs, macs=0, nbytes=0, scratch=(), in_specs=None, out_specs=None, aliases=None
):
    single = not isinstance(outs, list)
    return pl.pallas_call(
        body,
        in_specs=in_specs or [VMEM] * len(operands),
        out_specs=out_specs or (VMEM if single else [VMEM] * len(outs)),
        input_output_aliases=aliases or {},
        out_shape=outs,
        scratch_shapes=list(scratch),
        compiler_params=params(),
        cost_estimate=cost(macs, nbytes),
        name=name,
    )(*operands)


def pack(acc, out):
    blocks = acc.shape[1] // LANES
    for j in range(blocks):
        out[:, j, :] = acc[0:HALF, j * LANES : (j + 1) * LANES]
        out[:, blocks + j, :] = acc[HALF:K, j * LANES : (j + 1) * LANES]


def packed_shape(cols):
    return shape(HALF, 2 * cols // LANES, LANES)


def first_gradient(duals, returns):
    rows, cols = returns.shape
    steps = rows // TILE

    def body(u, r, out, mass, held, kept, acc, sems, dual_sems):
        copies = []
        for i in range(steps):
            at = pl.ds(i * TILE, TILE)
            mine = pltpu.make_async_copy(u.at[:, at], kept.at[:, at], dual_sems.at[i])
            block = pltpu.make_async_copy(r.at[at], held.at[at], sems.at[i])
            mine.start()
            block.start()
            copies.append((mine, block))
        folded = jnp.zeros((K, LANES), F32)
        for i in range(steps):
            copies[i][0].wait()
            part = kept[:, i * TILE : (i + 1) * TILE]
            folded = folded + lane_folded(part)
            copies[i][1].wait()
            term = jnp.dot(
                part.astype(BF16), held[pl.ds(i * TILE, TILE), :], preferred_element_type=F32
            )
            acc[...] = term if i == 0 else acc[...] + term
        pack(acc[...], out)
        mass[...] = in_lanes(row_total(folded))

    operands = [pltpu.with_memory_space_constraint(a, pltpu.HBM) for a in (duals, returns)]
    outs = [
        packed_shape(cols),
        shape(1, K),
        pltpu.VMEM((rows, cols), BF16),
        pltpu.VMEM((K, rows), F32),
    ]
    scratch = (
        pltpu.VMEM((K, cols), F32),
        pltpu.SemaphoreType.DMA((steps,)),
        pltpu.SemaphoreType.DMA((steps,)),
    )
    return call(
        body, "first_gradient", operands, outs, K * rows * cols, 2 * rows * cols, scratch, [ANY, ANY]
    )


def own_rows(received, state, extra, passed, first, total_cols, total_rows):
    scale = math.sqrt(total_cols / total_rows)
    cols = state.shape[1]
    blocks = cols // LANES
    lines = 2 * blocks

    def body(got, v, more, *refs):
        s = scen_index()
        grad = jnp.sum(got[...], 0)
        if first:
            out, line_out = refs
            for j in range(blocks):
                piece = more[pl.ds(j * LANES, LANES)].reshape(1, LANES)
                line_out[:, j * LANES : (j + 1) * LANES] = piece
                out[lines + j : lines + j + 1, :] = piece
                out[lines + blocks + j : lines + blocks + j + 1, :] = piece
        else:
            through, out, through_out = refs
            through_out[...] = through[...]
            out[lines:, :] = jnp.zeros((out.shape[0] - lines, LANES), F32)
            out[lines : lines + 1, 0:K] = more[...]
        for half in range(2):
            values = v[half * HALF : (half + 1) * HALF, :]
            at = lax.broadcasted_iota(jnp.int32, values.shape, 0) == s
            old = jnp.sum(jnp.where(at, values, 0.0), 0, keepdims=True)
            for j in range(blocks):
                line = half * blocks + j
                out[line : line + 1, :] = (
                    old[:, j * LANES : (j + 1) * LANES] + STEP_V * scale * grad[line : line + 1, :]
                )

    operands = (received, state, extra) + ((passed,) if passed is not None else ())
    outs = [shape(2 * lines, LANES), shape(1, cols)] if first else [shape(lines + 8, LANES)]
    if passed is not None:
        outs.append(shape(*passed.shape))
    return call(body, "own_rows", operands, outs, nbytes=4 * HALF * lines * LANES)


def projected(gathered, own, gathered_first, own_first, lam_old, goal, mass, first, total_cols):
    lines = gathered_first.shape[1] // 2
    blocks = lines // 2

    def body(rows, mine, means, mean, lam_in, target, sums_in, out, lam_out):
        s = scen_index()
        first_row = lax.broadcasted_iota(jnp.int32, (lines, LANES), 0) < blocks

        def folded(values):
            a = jnp.sum(jnp.where(first_row, values, 0.0), 0, keepdims=True)
            b = jnp.sum(jnp.where(first_row, 0.0, values), 0, keepdims=True)
            return jnp.concatenate([a, b], 0)

        def spread(pair):
            return jnp.where(first_row, pair[0:1, :], pair[1:2, :])

        lam = lam_in[...]
        if not first:
            ret = rows[0, lines : lines + 1, 0:K]
            for i in range(1, rows.shape[0]):
                ret = ret + rows[i, lines : lines + 1, 0:K]
            lam = jnp.maximum(lam + STEP_L * (target[...] - ret / total_cols), 0.0)
        lam_out[...] = lam
        slope = STEP_V * spread(jnp.concatenate([picked(lam, s), picked(lam, s + HALF)], 0))
        parts = [
            rows[i, 0:lines, :] + slope * means[i, lines : 2 * lines, :]
            for i in range(rows.shape[0])
        ]
        total = parts[0]
        top = parts[0]
        for part in parts[1:]:
            total = total + part
            top = jnp.maximum(top, part)
        low = jnp.min(top, 0, keepdims=True)
        top_a = jnp.max(jnp.where(first_row, top, low), 0, keepdims=True)
        top_b = jnp.max(jnp.where(first_row, low, top), 0, keepdims=True)
        upper = jnp.max(jnp.concatenate([top_a, top_b], 0), 1, keepdims=True)
        lower = jnp.sum(folded(total), 1, keepdims=True) / total_cols - 1.0

        def excesses(levels):
            found = []
            for level in levels:
                wide = spread(level)
                over = jnp.maximum(parts[0] - wide, 0.0)
                for part in parts[1:]:
                    over = over + jnp.maximum(part - wide, 0.0)
                found.append(folded(over))
            whole = jnp.sum(jnp.concatenate(found, 0), 1, keepdims=True) - total_cols
            return [whole[2 * i : 2 * i + 2, :] for i in range(len(levels))]

        def middles(bounds, depth):
            if depth == 0:
                return None
            low_end, high_end = bounds
            middle = (low_end + high_end) * 0.5
            return (
                middle,
                middles((low_end, middle), depth - 1),
                middles((middle, high_end), depth - 1),
            )

        def listed(tree):
            return [] if tree is None else [tree[0]] + listed(tree[1]) + listed(tree[2])

        def with_values(tree, values):
            if tree is None:
                return None
            return ((tree[0], values.pop(0)), with_values(tree[1], values), with_values(tree[2], values))

        def picked_tree(raise_low, above, below):
            if above is None:
                return None
            node = tuple(jnp.where(raise_low, a, b) for a, b in zip(above[0], below[0]))
            return (
                node,
                picked_tree(raise_low, above[1], below[1]),
                picked_tree(raise_low, above[2], below[2]),
            )

        f_low = None
        f_up = jnp.zeros_like(lower) - total_cols
        for _ in range(BISECT // AHEAD):
            tree = middles((lower, upper), AHEAD)
            levels = listed(tree)
            if f_low is None:
                f_low, *values = excesses([lower] + levels)
            else:
                values = excesses(levels)
            tree = with_values(tree, values)
            while tree is not None:
                (middle, excess), below, above = tree
                raise_low = excess >= 0
                lower = jnp.where(raise_low, middle, lower)
                upper = jnp.where(raise_low, upper, middle)
                f_low = jnp.where(raise_low, excess, f_low)
                f_up = jnp.where(raise_low, f_up, excess)
                tree = picked_tree(raise_low, above, below)
        theta = lower + f_low * (upper - lower) / (f_low - f_up)
        x = mine[0:lines, :] + slope * mean[lines : 2 * lines, :]
        fresh = jnp.maximum(x - spread(theta), 0.0)
        mass = jnp.concatenate([sums_in[...], jnp.zeros((1, LANES - K), F32)], 1)
        for i in range(HALF):
            for half in range(2):
                out[i, 0:blocks, half, :] = fresh[half * blocks : (half + 1) * blocks, :]
                out[i, blocks : blocks + 1, half, :] = mass

    return call(
        body,
        "projected",
        (gathered, own, gathered_first, own_first, lam_old, goal, mass),
        [shape(HALF, blocks + 1, 2, LANES), shape(1, K)],
        nbytes=4 * HALF * HALF * LANES,
    )


def unpacked(received, state, start, mean_row, t_old, last, total_rows):
    cols = state.shape[1]
    blocks = cols // LANES

    def body(got, v, w, m, t, fresh, bars, t_new, t_bar, ret):
        for j in range(blocks):
            at = slice(j * LANES, (j + 1) * LANES)
            fresh[0:HALF, at] = got[:, j, 0, :]
            fresh[HALF:K, at] = got[:, j, 1, :]
        mass = jnp.sum(got[:, blocks, 0, :], 0, keepdims=True)[:, 0:K]
        t_end = t[...] - STEP_T * (1.0 - mass / total_rows / TAIL)
        t_new[...] = t_end
        t_bar[...] = jnp.broadcast_to(in_rows(2.0 * t_end - t[...]), (K, LANES))
        bar = 2.0 * fresh[...] - v[...]
        bars[0:K, :] = (-bar).astype(BF16)
        if not last:
            bars[K : 2 * K, :] = (-w[...]).astype(BF16)
        ret[...] = in_lanes(row_total(lane_folded(bar * m[...])))

    outs = [
        shape(K, cols),
        shape((1 if last else 2) * K, cols, dtype=BF16),
        shape(1, K),
        shape(K, LANES),
        shape(1, K),
    ]
    return call(
        body, "unpacked", (received, state, start, mean_row, t_old), outs, nbytes=20 * K * cols
    )


def mixed(fresh, old, start):
    return (2.0 / 3.0) * (2.0 * fresh - old) + start / 3.0


def averaged(weights, thresholds):
    def body(v2, v1, v0, t2, t1, t0, v_out, t_out):
        v_out[...] = mixed(v2[...], v1[...], v0[...])
        t_out[...] = mixed(t2[...], t1[...], t0[...])

    outs = [shape(*weights[0].shape), shape(1, K)]
    return call(
        body, "averaged", (*weights, *thresholds), outs, nbytes=16 * weights[0].size
    )


def loss_part(bars, returns, sides, quarter, width):
    cols = returns.shape[1]
    count = bars.shape[0] // K

    def body(b, r, *outs):
        for index, side in enumerate(sides):
            base = row_base(side, quarter(), width)
            for i in range(width // TILE):
                at = slice(i * TILE, (i + 1) * TILE)
                block = r[pl.ds(start_of(base + i * TILE), TILE), :]
                term = lax.dot_general(
                    block, b[...], (((1,), (1,)), ((), ())), preferred_element_type=F32
                ).T
                for part in range(count):
                    outs[index * count + part][:, at] = term[part * K : (part + 1) * K, :]

    outs = [shape(K, width)] * (count * len(sides))
    return call(
        body,
        "loss_part",
        (bars, returns),
        outs,
        len(outs) * K * width * cols,
        2 * len(sides) * width * cols,
    )


def plus(a, b, pieces=1):
    rows = a.shape[0] // pieces

    def body(x, y, *outs):
        for i, out in enumerate(outs):
            at = slice(i * rows, (i + 1) * rows)
            out[...] = x[at, :] + y[at, :]

    outs = [shape(rows, a.shape[1])] * pieces
    return call(body, "plus", (a, b), outs, nbytes=12 * a.size)


def own_and_other(keeps, takes):
    def body(k0, t0, k1, t1, send, keep):
        near = k0[...] + t0[...]
        far = k1[...] + t1[...]
        swap = lax.axis_index("xh") == 0
        send[...] = jnp.where(swap, far, near)
        keep[...] = jnp.where(swap, near, far)

    return call(
        body,
        "own_and_other",
        (keeps[0], takes[0], keeps[1], takes[1]),
        [shape(*keeps[0].shape)] * 2,
        nbytes=24 * keeps[0].size,
    )


def dual_step(loss, duals, t_bar):
    return jnp.clip(duals + STEP_U * (loss - t_bar[:, 0:1]), 0.0, 1.0)


def dual_row(parts, others, duals, t_bar, quarter, width):
    count = len(parts)
    rows = K // count

    def body(*refs):
        u, t, fresh = refs[2 * count :]
        base = row_base(1, quarter, width)
        for i in range(count):
            at = slice(i * rows, (i + 1) * rows)
            loss = refs[i][...] + refs[count + i][...]
            fresh[at, :] = dual_step(loss, u[at, pl.ds(base, width)], t[at, :])

    operands = (*parts, *others, duals, t_bar)
    return call(body, "dual_row", operands, shape(K, width), nbytes=16 * K * width)


def gradient_part(terms, returns, before, width):
    cols = returns.shape[1]
    count = len(terms)

    def body(r, *refs):
        fed, rest = refs[:count], refs[count:]
        acc_out, folded_out = rest[-2:]
        total = rest[0][...] if before else None
        folds = rest[1][...] if before else None
        for (_, side, quarter), ref in zip(terms, fed):
            base = row_base(side, quarter, width)
            value = ref[...]
            term = jnp.dot(
                value.astype(BF16), r[pl.ds(base, width), :], preferred_element_type=F32
            )
            total = term if total is None else total + term
            fold = lane_folded(value)
            folds = fold if folds is None else folds + fold
        acc_out[...] = total
        folded_out[...] = folds

    operands = [returns] + [values for values, _, _ in terms] + list(before)
    return call(
        body,
        "gradient_part",
        operands,
        [shape(K, cols), shape(K, LANES)],
        count * K * width * cols,
        2 * count * width * cols,
    )


def gradient_end(taken, side, quarter, returns, before, width):
    cols = returns.shape[1]

    def body(r, got, acc_in, folded_in, out, mass):
        base = row_base(side, quarter, width)
        term = acc_in[...] + jnp.dot(
            got[...].astype(BF16), r[pl.ds(base, width), :], preferred_element_type=F32
        )
        pack(term, out)
        mass[...] = in_lanes(row_total(folded_in[...] + lane_folded(got[...])))

    return call(
        body,
        "gradient_end",
        (returns, taken, *before),
        [packed_shape(cols), shape(1, K)],
        K * width * cols,
        2 * width * cols,
    )


def final_duals(part, other, tails, held, start, t_new, t_old, t_start, t_bar, ret, width):
    devices = 128

    def body(p, o, la, lb, ua, ub, u0, tn, t, ts, tb, er, duals_out, sums):
        mine = lax.axis_index("xh")
        base = row_base(1, mine, width)
        loss = p[...] + o[...]
        old = jnp.where(mine == 0, ua[...], ub[...])
        fresh = dual_step(loss, old, tb[...])
        duals_out[...] = mixed(fresh, old, u0[:, pl.ds(base, width)])
        end = mixed(tn[...], t[...], ts[...])
        tail = (2.0 / 3.0) * loss + (la[...] + lb[...]) / 3.0
        over = jnp.maximum(tail - in_rows(end), 0.0)
        line = jnp.concatenate([in_lanes(row_total(lane_folded(over))), er[...]], 1)
        sums[...] = jnp.broadcast_to(line[None], (devices, 1, LANES))

    operands = (part, other, *tails, *held, start, t_new, t_old, t_start, t_bar, ret)
    return call(
        body,
        "final_duals",
        operands,
        [shape(K, width), shape(devices, 1, LANES)],
        nbytes=24 * K * width,
    )


def joined(pieces, width, ends, total_cols, total_rows):
    devices = ends[0].shape[0]
    copies_of_ret = devices // 4

    def body(
        near, far, own, got, t2, t1, t0, lam_1, lam_0, target, out, tail_out, lam_out, tail, lam, sems
    ):
        mine = lax.axis_index("xh")
        places = ((1, 1 - mine, near), (0, mine, far), (1, mine, own))
        copies = []
        for i, (side, quarter, ref) in enumerate(places):
            to = out.at[:, pl.ds(row_base(side, quarter, width), width)]
            copies.append(pltpu.make_async_copy(ref, to, sems.at[i]))
        for copy in copies:
            copy.start()
        total = jnp.sum(got[...], 0)
        end = mixed(t2[...], t1[...], t0[...])
        tail[...] = end + total[:, 0:K] / (TAIL * total_rows)
        ret = total[:, K : 2 * K] / copies_of_ret
        fresh = jnp.maximum(lam_1[...] + STEP_L * (target[...] - ret / total_cols), 0.0)
        lam[...] = mixed(fresh, lam_1[...], lam_0[...])
        for ref, to in ((tail, tail_out), (lam, lam_out)):
            copies.append(pltpu.make_async_copy(ref, to, sems.at[len(copies)]))
            copies[-1].start()
        for copy in copies:
            copy.wait()

    return call(
        body,
        "joined",
        (*pieces, *ends),
        [pltpu.HBM((K, 4 * width), F32), pltpu.HBM((1, K), F32), pltpu.HBM((1, K), F32)],
        nbytes=24 * K * width,
        scratch=(
            pltpu.VMEM((1, K), F32),
            pltpu.VMEM((1, K), F32),
            pltpu.SemaphoreType.DMA((5,)),
        ),
        out_specs=[ANY] * 3,
    )


def completed(duals_out, last, width):
    def body(before, piece, out, sem):
        to = out.at[:, pl.ds(row_base(0, 1 - lax.axis_index("xh"), width), width)]
        copy = pltpu.make_async_copy(piece, to, sem)
        copy.start()
        copy.wait()

    return call(
        body,
        "completed",
        (duals_out, last),
        pltpu.HBM(duals_out.shape, F32),
        nbytes=8 * K * width,
        scratch=(pltpu.SemaphoreType.DMA,),
        in_specs=[ANY, VMEM],
        out_specs=ANY,
        aliases={0: 0},
    )


def pinned(a):
    return pltpu.with_memory_space_constraint(a, pltpu.VMEM)


def across(values, axis):
    return lax.ppermute(values, axis, [(0, 1), (1, 0)])


def plus_gathered(a, both, pieces=1):
    rows = a.shape[0] // pieces

    def body(x, y, *outs):
        other = 1 - lax.axis_index("core")
        for i, out in enumerate(outs):
            at = slice(i * rows, (i + 1) * rows)
            out[...] = x[at, :] + y[other, at, :]

    outs = [shape(rows, a.shape[1])] * pieces
    return call(body, "plus", (a, both), outs, nbytes=12 * a.size)


def exchanged(payload, others):
    payload, others = lax.optimization_barrier((payload, others))
    received = lax.all_to_all(payload, SCEN, 0, 0)
    return lax.optimization_barrier((received, others))


def local(returns, mean_return, targets, weights, threshold, duals, multiplier):
    scen_rows, cols = returns.shape
    total_cols = cols * 4
    total_rows = scen_rows * 32
    width = scen_rows // 4
    t0 = threshold.reshape(1, K)
    lam0 = multiplier.reshape(1, K)
    goal = targets.reshape(1, K)

    payload, mass, returns, duals = first_gradient(duals, returns)
    returns = pinned(returns)
    held = (returns, duals, weights, mean_return, t0, lam0, goal, mass)
    received, held = exchanged(payload, held)
    returns, duals, weights, mean_return, t0, lam0, goal, mass = held
    own_first, mean_row = own_rows(
        received, weights, mean_return, None, True, total_cols, total_rows
    )
    gathered_first = lax.all_gather(own_first, ASSET)
    payload, lam0 = projected(
        gathered_first, own_first, gathered_first, own_first, lam0, goal, mass, True, total_cols
    )
    held = (returns, duals, weights, mean_row, t0, lam0, goal, gathered_first, own_first)
    received, held = exchanged(payload, held)
    returns, duals, weights, mean_row, t0, lam0, goal, gathered_first, own_first = held
    returns = pinned(returns)
    v1, bars, t1, bar1, ret1 = unpacked(
        received, weights, weights, mean_row, t0, False, total_rows
    )

    send, send_tail_a = loss_part(bars, returns, (0,), lambda: 0, width)
    take = across(send, "core")
    keep, keep_tail_a = loss_part(bars, returns, (1,), lambda: 0, width)
    part_a = plus(keep, take, 1)
    take_tail_a = across(send_tail_a, "core")
    part_a, bars = lax.optimization_barrier((part_a, bars))
    send, send_tail_b, keep, keep_tail_b = loss_part(bars, returns, (0, 1), lambda: 1, width)
    part_b = plus_gathered(keep, lax.all_gather(send, "core"), 2)
    take_tail_b = across(send_tail_b, "core")
    others = [[across(piece, "xh") for piece in part] for part in (part_a, part_b)]
    send_tail, tail_a = own_and_other((keep_tail_a, keep_tail_b), (take_tail_a, take_tail_b))

    ua = dual_row(part_a, others[0], duals, bar1, 0, width)
    taken_a = across(ua, "core")
    ub = dual_row(part_b, others[1], duals, bar1, 1, width)
    ub, send_tail = lax.optimization_barrier((ub, send_tail))
    taken_b = across(ub, "core")
    sums = gradient_part([(ua, 1, 0), (ub, 1, 1)], returns, (), width)
    sums = gradient_part([(taken_a, 0, 0)], returns, sums, width)
    payload, mass = gradient_end(taken_b, 0, 1, returns, sums, width)

    held = (returns, duals, weights, mean_row, v1, t0, t1, lam0, goal, gathered_first, own_first)
    held = held + (ret1, ua, ub, tail_a, send_tail, mass)
    received, held = exchanged(payload, held)
    returns, duals, weights, mean_row, v1, t0, t1, lam0, goal, gathered_first, own_first = held[:11]
    ret1, ua, ub, tail_a, send_tail, mass = held[11:]
    own, send_tail = own_rows(received, v1, ret1, send_tail, False, total_cols, total_rows)
    tail_b = across(send_tail, "xh")
    gathered = lax.all_gather(own, ASSET)
    payload, lam1 = projected(
        gathered, own, gathered_first, own_first, lam0, goal, mass, False, total_cols
    )
    held = (returns, duals, weights, mean_row, v1, t0, t1, lam0, lam1, goal, ua, ub, tail_a, tail_b)
    received, held = exchanged(payload, held)
    returns, duals, weights, mean_row, v1, t0, t1, lam0, lam1, goal, ua, ub, tail_a, tail_b = held
    returns = pinned(returns)
    v2, bars, t2, bar2, ret2 = unpacked(received, v1, weights, mean_row, t1, True, total_rows)

    def far_quarter():
        return 1 - lax.axis_index("xh")

    def own_quarter():
        return lax.axis_index("xh")

    (send,) = loss_part(bars, returns, (0,), far_quarter, width)
    take = across(send, "core")
    (keep,) = loss_part(bars, returns, (1,), far_quarter, width)
    (part_a,) = plus(keep, take)
    part_a, bars, v2 = lax.optimization_barrier((part_a, bars, v2))
    send, keep = loss_part(bars, returns, (0, 1), own_quarter, width)
    (part_b,) = plus_gathered(keep, lax.all_gather(send, "core"))
    parts = (part_a, part_b)
    other = across(parts[0], "xh")
    weights_out, threshold_out = averaged((v2, v1, weights), (t2, t1, t0))
    part, weights_out = lax.optimization_barrier((parts[1], weights_out))

    quarter, sums = final_duals(
        part, other, (tail_a, tail_b), (ua, ub), duals, t2, t1, t0, bar2, ret2, width
    )
    near = across(quarter, "xh")
    far = across(quarter, "core")
    sums = lax.all_to_all(sums, ALL, 0, 0)
    near, far, sums = lax.optimization_barrier((near, far, sums))
    far_near = across(near, "core")
    ends = (sums, t2, t1, t0, lam1, lam0, goal)
    duals_out, tail_risk, lam_out = joined(
        (near, far, quarter), width, ends, total_cols, total_rows
    )
    duals_out = completed(duals_out, far_near, width)
    return (weights_out, threshold_out.reshape(K), duals_out, lam_out.reshape(K), tail_risk.reshape(K))


def solution(mesh):
    split = Mesh(mesh.devices.reshape(4, 4, 2, 2, 2), ALL)
    in_specs = (P(SCEN, ASSET), P(ASSET), P(), P(None, ASSET), P(), P(None, SCEN), P())
    out_specs = (P(None, ASSET), P(), P(None, SCEN), P(), P())
    return jax.shard_map(local, mesh=split, in_specs=in_specs, out_specs=out_specs, check_vma=False)
```
